32 devices in a mesh: sec: 4 (over y, x), xs: 8 (over z, core).
Axes of the slice: x: 2, y: 2, z: 4, core: 2. Of those that a mesh axis runs over, the one named last changes fastest.
Arguments:
- soot: float32 [96, 128, 1024], P('sec', 'xs'), may hold values from 0.05 to 1
- species: float32 [40, 128, 1024], P(None, 'xs'), may hold values from 0.1 to 1
- kernel: float32 [96, 96], replicated, may hold values from 0.002 to 0.02
- split: float32 [96, 96], replicated, may hold values from 0.2 to 0.8
- target: int32 [96, 96], replicated, may hold values from 0 to 94, as said below
- growth: float32 [96], replicated, may hold values from 0.05 to 0.5
- diffusivity: float32 [40], replicated, may hold values from 0.05 to 0.2
- reaction: float32 [40, 40], replicated, may hold values from -1 to 1
- stoich: float32 [40], replicated, may hold values from -1 to 1
Outputs:
- soot_out: float32 [96, 128, 1024], P('sec', 'xs')
- species_out: float32 [40, 128, 1024], P(None, 'xs')
The draws below stay inside these ranges and needn't reach their ends.
Inputs may be any that keep to these rules, and one draw needn't show every extreme that they name: target[i, j] = min(max(i, j) + r, 94) with r of 0 to 3.
All inputs are finite; a program needn't handle non-finite values.
Results may differ from the reference program's by a relative error of at most 0.0003.
Values sent between devices are 32-bit elements; how exact they have to be, the bound alone decides.
No kernel may reach another device: no remote copies, remote signals or barrier semaphores. Data moves between devices by JAX's collectives and lax.ppermute only.
A program may use at most 128 MiB of HBM per device.

```python
import math
import jax
import jax.numpy as jnp
from jax import lax

S = 96
K = 40
CZ = 1024
NY = 128


def draw_target(key, part):
    rows = jnp.arange(S, dtype=jnp.int32)
    larger = jnp.maximum(rows[:, None], rows[None, :])
    offset = jax.random.randint(key, (S, S), 0, 4, dtype=jnp.int32)
    return jnp.minimum(larger + offset, S - 2).astype(jnp.int32)


def shard_levels(stream_key, dims, shards, smallest, largest):
    level = 1.0
    for axis_at, shards_of in shards:
        steps = jax.random.uniform(jax.random.fold_in(jax.random.fold_in(stream_key, 6), axis_at), (shards_of,), jnp.float32, smallest / len(shards), largest / len(shards))
        level = level * jnp.repeat(jnp.exp(steps), dims[axis_at] // shards_of).reshape((-1,) + (1,) * (len(dims) - 1 - axis_at))
    return level


def normal_values(own_key, extent, spread, limit, held_as=jnp.bfloat16):
    return jnp.clip(spread * jax.random.normal(own_key, extent, jnp.float32), -limit, limit).astype(held_as)


def setup_inputs(seed: int = 0) -> dict:
    key_list = jax.random.split(jax.random.key(seed), 10)
    return {
        "soot": jnp.clip(jnp.exp(math.log(1.0) - 2.9957323 * jax.random.uniform(key_list[0], (S, NY, CZ), jnp.float32) ** shard_levels(key_list[0], (S, NY, CZ), ((0, 4), (1, 8)), -0.2, 0.2)), 0.05, 1.0),
        "species": jnp.clip(jnp.exp(math.log(1.0) - 2.3025851 * jax.random.uniform(key_list[1], (K, NY, CZ), jnp.float32) ** shard_levels(key_list[1], (K, NY, CZ), ((1, 8),), -0.2, 0.2)), 0.1, 1.0),
        "kernel": jnp.clip(jnp.exp(jax.random.uniform(key_list[2], (S, S), jnp.float32, math.log(0.002), math.log(0.02))), 0.002, 0.02),
        "split": jnp.clip(jax.random.uniform(key_list[3], (S, S), jnp.float32, 0.2, 0.8), 0.2, 0.8),
        "target": draw_target(jax.random.fold_in(key_list[9], 71), 0),
        "growth": jnp.clip(jnp.exp(jax.random.uniform(key_list[5], (S,), jnp.float32, math.log(0.05), math.log(0.5))), 0.05, 0.5),
        "diffusivity": jnp.clip(jax.random.uniform(key_list[6], (K,), jnp.float32, 0.05, 0.2), 0.05, 0.2),
        "reaction": normal_values(key_list[7], (K, K), K ** -0.5, 1.0, jnp.float32),
        "stoich": jnp.clip(jax.random.uniform(key_list[8], (K,), jnp.float32, -1.0, 1.0), -1.0, 1.0),
    }


HI = lax.Precision.HIGHEST


def laplace(field):
    padded = jnp.pad(field, ((0, 0), (1, 1), (1, 1)))
    beside = padded[:, 2:, 1:-1] + padded[:, :-2, 1:-1] + padded[:, 1:-1, 2:] + padded[:, 1:-1, :-2]
    return beside - 4.0 * field


def birth_rows(dense, kernel, split, target, first, count):
    def one_target(index):
        weights = 0.5 * kernel * (split * (target == index).astype(kernel.dtype) + (1.0 - split) * (target + 1 == index).astype(kernel.dtype))
        product = jnp.dot(weights, dense, precision=HI)
        return jnp.sum(dense * product, axis=0)
    indices = (first + jnp.arange(count)).astype(jnp.int32)
    return lax.map(one_target, indices)


def reference(soot, species, kernel, split, target, growth, diffusivity, reaction, stoich):
    cells = soot.shape[1] * soot.shape[2]
    dense = soot.reshape(S, cells)
    acet = species[0].reshape(1, cells)
    birth = birth_rows(dense, kernel, split, target, 0, S)
    loss = dense * jnp.dot(kernel, dense, precision=HI)
    flux = growth[:, None] * dense * acet
    inflow = jnp.concatenate([jnp.zeros((1, cells), dense.dtype), flux[:-1]], axis=0)
    consumption = jnp.sum(flux, axis=0)
    rate = (birth - loss - flux + inflow).reshape(soot.shape)
    soot_out = soot + 0.1 * laplace(soot) + rate
    mixed = jnp.dot(reaction, species.reshape(K, cells), precision=HI).reshape(species.shape)
    species_out = species + diffusivity[:, None, None] * laplace(species) + mixed - stoich[:, None, None] * consumption.reshape(1, soot.shape[1], soot.shape[2])
    return soot_out, species_out
```

```python
import functools

import jax
import jax.numpy as jnp
from jax import lax
from jax.experimental import pallas as pl
from jax.experimental.pallas import tpu as pltpu
from jax.sharding import PartitionSpec as P

F32 = jnp.float32
BF16 = jnp.bfloat16
SUB = 8
LANE = 128
SHIFTS = 5
ANY = pl.BlockSpec(memory_space=pl.ANY)
VMEM = pl.BlockSpec(memory_space=pltpu.VMEM)
SMEM = pl.BlockSpec(memory_space=pltpu.SMEM)
PARAMS = pltpu.CompilerParams(vmem_limit_bytes=48 * 1024 * 1024)


def halves(x):
    high = x.astype(BF16)
    return high, (x - high.astype(F32)).astype(BF16)


class Plan:
    def __init__(self, n, rows, width):
        self.n = n
        self.across = min(n, width // LANE)
        self.down = n // self.across
        self.rows = rows // self.down
        self.cols = width // self.across
        self.chunks = self.rows // SUB

    def place(self, owner, chunk):
        row = (owner // self.across) * self.rows + chunk * SUB
        col = (owner % self.across) * self.cols
        return pl.ds(pl.multiple_of(row, SUB), SUB), pl.ds(pl.multiple_of(col, LANE), self.cols)


def peer(k):
    return lax.axis_index("sec") ^ k


def cut_kernel(plan, soot, *rest):
    outs, sems = rest[:-1], rest[-1]
    copies = []
    for chunk in range(plan.chunks):
        for k in range(plan.n):
            at = chunk * plan.n + k
            rows, cols = plan.place(peer(k), chunk)
            copies.append(pltpu.make_async_copy(soot.at[:, rows, cols], outs[at], sems.at[at]))
            copies[-1].start()
    for copy in copies:
        copy.wait()


def cut(plan, soot):
    count = plan.chunks * plan.n
    shape = jax.ShapeDtypeStruct((soot.shape[0], SUB, plan.cols), F32)
    return pl.pallas_call(
        functools.partial(cut_kernel, plan),
        out_shape=[shape] * count,
        in_specs=[ANY],
        out_specs=[VMEM] * count,
        scratch_shapes=[pltpu.SemaphoreType.DMA((count,))],
        compiler_params=PARAMS,
        name="cut",
    )(soot)


def edge_kernel(soot, species, head, tail):
    local, rows, _ = soot.shape
    for ref, at in ((soot, 0), (species, local)):
        count = ref.shape[0]
        for out, row in ((head, 0), (tail, rows - 1)):
            out[at : at + count, :] = ref[:, row, :]


def edges(soot, species):
    shape = jax.ShapeDtypeStruct((soot.shape[0] + species.shape[0], soot.shape[2]), F32)
    return pl.pallas_call(
        edge_kernel,
        out_shape=[shape, shape],
        in_specs=[VMEM, VMEM],
        out_specs=[VMEM, VMEM],
        compiler_params=PARAMS,
        name="edges",
    )(soot, species)


def weight_kernel(kernel, split, target, growth, twice, rest, rate, rate_before, scratch):
    size = kernel.shape[0]
    row = lax.broadcasted_iota(jnp.int32, (size, size), 0)
    col = lax.broadcasted_iota(jnp.int32, (size, size), 1)
    k, sp = kernel[...], split[...]
    t = target[...].astype(F32)
    rowf = row.astype(F32)
    k_t, sp_t, t_t = k.T, sp.T, t.T
    low, high = 0.5 * k * sp, 0.5 * k * (1.0 - sp)
    low_t, high_t = 0.5 * k_t * sp_t, 0.5 * k_t * (1.0 - sp_t)

    def fed(shift):
        at = rowf + shift
        own = jnp.where(t == at, low, 0.0) + jnp.where(t + 1.0 == at, high, 0.0)
        other = jnp.where(t_t == at, low_t, 0.0) + jnp.where(t_t + 1.0 == at, high_t, 0.0)
        return jnp.where(col <= row, own, 0.0) + jnp.where(col < row, other, 0.0)

    scratch[...] = jnp.zeros_like(scratch)
    scratch[0:size, :] = fed(0) - k
    for shift in range(1, SHIFTS):
        scratch[shift * size + shift : (shift + 1) * size, :] = fed(shift)[: size - shift]
    last = SHIFTS * size
    scratch[last : last + SUB - 1, :] = fed(-1)[size - SUB + 1 :]
    w_high, w_low = halves(scratch[...])
    twice[:, :size] = w_high
    twice[:, size:] = w_high
    rest[...] = w_low
    diagonal = jnp.where(row == col, jnp.broadcast_to(growth[...], (size, size)), 0.0)
    column = jnp.sum(diagonal, axis=1, keepdims=True)
    rate[...] = jnp.broadcast_to(column, rate.shape)
    before = jnp.where(row == col + 1, jnp.broadcast_to(growth[...], (size, size)), 0.0)
    column = jnp.sum(before, axis=1, keepdims=True)
    rate_before[...] = jnp.broadcast_to(column, rate_before.shape)


def weights(plan, kernel, split, target, growth):
    size = kernel.shape[0]
    depth = SHIFTS * size + 2 * SUB
    return pl.pallas_call(
        weight_kernel,
        out_shape=[
            jax.ShapeDtypeStruct((depth, 2 * size), BF16),
            jax.ShapeDtypeStruct((depth, size), BF16),
            jax.ShapeDtypeStruct((size, plan.cols), F32),
            jax.ShapeDtypeStruct((size, plan.cols), F32),
        ],
        in_specs=[VMEM] * 4,
        out_specs=[VMEM] * 4,
        scratch_shapes=[pltpu.VMEM((depth, size), F32)],
        compiler_params=PARAMS,
        name="weights",
    )(kernel, split, target, growth.reshape(1, size))


def rate_kernel(plan, chunk, twice, rest, rate, rate_before, acet, *refs):
    n = plan.n
    pieces, outs = refs[:n], refs[n : 2 * n]
    whole, result, near, sem = refs[2 * n :]
    size = rate.shape[0]
    local = size // n
    rows, cols = plan.place(lax.axis_index("sec"), chunk)
    copy = pltpu.make_async_copy(acet.at[0, rows, cols], near, sem)
    copy.start()
    pad = SHIFTS - 1
    blocks = range(plan.cols // LANE)
    lanes = [slice(b * LANE, (b + 1) * LANE) for b in blocks]
    for b in blocks:
        whole[b, : pad * SUB, :] = jnp.zeros((pad * SUB, LANE), F32)
        whole[b, (pad + size) * SUB :, :] = jnp.zeros((SUB, LANE), F32)
        for k in range(n):
            start = pl.multiple_of((pad + local * peer(k)) * SUB, SUB)
            whole[b, pl.ds(start, local * SUB), :] = pieces[k][:, lanes[b]]
    copy.wait()

    def sections(first, count, row):
        parts = [whole[b, pl.ds((pad + first) * SUB + row, count, stride=SUB), :] for b in blocks]
        return jnp.concatenate(parts, axis=1)

    for row in range(SUB):
        here = sections(0, size, row)
        high, low = halves(here)
        product = jnp.dot(twice[...], jnp.concatenate([high, low], axis=0), preferred_element_type=F32)
        product += jnp.dot(rest[...], high, preferred_element_type=F32)
        total = here * product[:size]
        for shift in range(1, SHIFTS):
            total += sections(-shift, size, row) * product[shift * size : (shift + 1) * size]
        last = SHIFTS * size
        extra = sections(size - SUB + 1, SUB, row) * product[last : last + SUB]
        total = jnp.concatenate([total[: size - SUB], total[size - SUB :] + extra], axis=0)
        growing = near[row : row + 1, :]
        grown = rate[...] * here
        total -= growing * (grown - rate_before[...] * sections(-1, size, row))
        for b in blocks:
            result[b, pl.ds(row, size, stride=SUB), :] = total[:, lanes[b]]
        used = growing * jnp.sum(grown, axis=0, keepdims=True)
        for k in range(n):
            outs[k][local * SUB + row : local * SUB + row + 1, :] = used
    for k in range(n):
        start = pl.multiple_of(local * peer(k) * SUB, SUB)
        for b in blocks:
            outs[k][: local * SUB, lanes[b]] = result[b, pl.ds(start, local * SUB), :]


def rates(plan, chunk, prepared, acet, pieces):
    size = prepared[2].shape[0]
    local = size // plan.n
    shape = jax.ShapeDtypeStruct(((local + 1) * SUB, plan.cols), F32)
    outs = pl.pallas_call(
        functools.partial(rate_kernel, plan, chunk),
        out_shape=[shape] * plan.n,
        in_specs=[VMEM] * 4 + [ANY] + [VMEM] * plan.n,
        out_specs=[VMEM] * plan.n,
        scratch_shapes=[
            pltpu.VMEM((plan.cols // LANE, (SHIFTS + size) * SUB, LANE), F32),
            pltpu.VMEM((plan.cols // LANE, size * SUB, LANE), F32),
            pltpu.VMEM((SUB, plan.cols), F32),
            pltpu.SemaphoreType.DMA,
        ],
        compiler_params=PARAMS,
        name="rates",
    )(*prepared, acet, *[p.reshape(local * SUB, plan.cols) for p in pieces])
    return outs


def base_kernel(above, below, diffusivity, reaction, soot, species, soot_base, species_base, stack, mixed):
    local, rows, width = soot.shape
    kinds = species.shape[0]
    lanes = lax.broadcasted_iota(jnp.int32, (rows, width), 1)
    blocks = range(width // LANE)

    def spread(v, at, factor):
        up = jnp.concatenate([above[pl.ds(at, 1), :], v[:-1]], axis=0)
        down = jnp.concatenate([v[1:], below[pl.ds(at, 1), :]], axis=0)
        left = jnp.where(lanes == 0, 0.0, pltpu.roll(v, 1, 1))
        right = jnp.where(lanes == width - 1, 0.0, pltpu.roll(v, width - 1, 1))
        return v + factor * (up + down + left + right - 4.0 * v)

    def one_section(i, carry):
        soot_base[i] = spread(soot[i], i, 0.1)
        return carry

    lax.fori_loop(0, local, one_section, 0)
    for b in blocks:
        stack[b] = species[:, :, b * LANE : (b + 1) * LANE].reshape(kinds * rows, LANE)
    r_high, r_low = halves(reaction[...])
    r_all = jnp.concatenate([r_high.astype(F32), r_high.astype(F32), r_low.astype(F32)], axis=1).astype(BF16)
    for row in range(rows):
        at = pl.ds(row, kinds, stride=rows)
        v = jnp.concatenate([stack[b, at, :] for b in blocks], axis=1)
        high, low = halves(v)
        high, low = high.astype(F32), low.astype(F32)
        v_all = jnp.concatenate([high, low, high], axis=0).astype(BF16)
        product = jnp.dot(r_all, v_all, preferred_element_type=F32)
        for b in blocks:
            mixed[b, at, :] = product[:, b * LANE : (b + 1) * LANE]

    def one_species(i, carry):
        at = pl.ds(pl.multiple_of(i * rows, SUB), rows)
        more = jnp.concatenate([mixed[b, at, :] for b in blocks], axis=1)
        species_base[i] = spread(species[i], local + i, diffusivity[i]) + more
        return carry

    lax.fori_loop(0, kinds, one_species, 0)


def bases(above, below, diffusivity, reaction, soot, species):
    return pl.pallas_call(
        base_kernel,
        out_shape=[jax.ShapeDtypeStruct(soot.shape, F32), jax.ShapeDtypeStruct(species.shape, F32)],
        in_specs=[VMEM, VMEM, SMEM, VMEM, VMEM, VMEM],
        out_specs=[VMEM, VMEM],
        scratch_shapes=[pltpu.VMEM((soot.shape[2] // LANE, species.shape[0] * soot.shape[1], LANE), F32)] * 2,
        compiler_params=PARAMS,
        name="bases",
    )(above, below, diffusivity, reaction, soot, species)


def last_kernel(plan, stoich, soot_base, species_base, *refs):
    count = plan.n * plan.chunks
    pieces, (soot_out, species_out) = refs[:count], refs[count:]
    local, kinds = soot_out.shape[0], species_out.shape[0]
    for chunk in range(plan.chunks):
        for k in range(plan.n):
            piece = pieces[chunk * plan.n + k]
            rows, cols = plan.place(peer(k), chunk)
            soot_out[:, rows, cols] = soot_base[:, rows, cols] + piece[:local]
            used = piece[local]
            for kind in range(kinds):
                species_out[kind, rows, cols] = species_base[kind, rows, cols] - stoich[kind] * used


def last(plan, stoich, soot_base, species_base, pieces):
    local = soot_base.shape[0]
    return pl.pallas_call(
        functools.partial(last_kernel, plan),
        out_shape=[jax.ShapeDtypeStruct(soot_base.shape, F32), jax.ShapeDtypeStruct(species_base.shape, F32)],
        in_specs=[SMEM, VMEM, VMEM] + [VMEM] * len(pieces),
        out_specs=[VMEM, VMEM],
        compiler_params=PARAMS,
        name="last",
    )(stoich, soot_base, species_base, *[p.reshape(local + 1, SUB, plan.cols) for p in pieces])


def shards(soot, species, kernel, split, target, growth, diffusivity, reaction, stoich):
    n = lax.axis_size("sec")
    plan = Plan(n, soot.shape[1], soot.shape[2])

    def swap(x, k):
        return lax.ppermute(x, "sec", [(i, i ^ k) for i in range(n)]) if k else x

    sent = cut(plan, soot)
    got = [[swap(sent[chunk * n + k], k) for k in range(n)] for chunk in range(plan.chunks)]
    head, tail = edges(soot, species)
    count = lax.axis_size("xs")
    above = lax.ppermute(tail, "xs", [(i, i + 1) for i in range(count - 1)])
    below = lax.ppermute(head, "xs", [(i + 1, i) for i in range(count - 1)])
    prepared = weights(plan, kernel, split, target, growth)
    soot_base, species_base = bases(above, below, diffusivity, reaction, soot, species)
    back = []
    for chunk in range(plan.chunks):
        outs = rates(plan, chunk, prepared, species, got[chunk])
        back += [swap(outs[k], k) for k in range(n)]
    return tuple(last(plan, stoich, soot_base, species_base, back))


def solution(mesh):
    return jax.shard_map(
        shards,
        mesh=mesh,
        in_specs=(P("sec", "xs", None), P(None, "xs", None), P(), P(), P(), P(), P(), P(), P()),
        out_specs=(P("sec", "xs", None), P(None, "xs", None)),
        check_vma=False,
    )
```

```python
import functools

import jax
import jax.numpy as jnp
from jax import lax
from jax.experimental import pallas as pl
from jax.experimental.pallas import tpu as pltpu
from jax.sharding import PartitionSpec as P

F32 = jnp.float32
BF16 = jnp.bfloat16
SUB = 8
LANE = 128
SHIFTS = 5
ANY = pl.BlockSpec(memory_space=pl.ANY)
VMEM = pl.BlockSpec(memory_space=pltpu.VMEM)
SMEM = pl.BlockSpec(memory_space=pltpu.SMEM)
HBM = pl.BlockSpec(memory_space=pltpu.HBM)
PARAMS = pltpu.CompilerParams(vmem_limit_bytes=16 * 1024 * 1024)


def halves(x):
    high = x.astype(BF16)
    return high, (x - high.astype(F32)).astype(BF16)


class Plan:
    def __init__(self, n, rows, width):
        self.n = n
        self.across = min(n, width // LANE)
        self.down = n // self.across
        self.rows = rows // self.down
        self.cols = width // self.across
        self.chunks = self.rows // SUB

    def whole(self, owner):
        row = (owner // self.across) * self.rows
        col = (owner % self.across) * self.cols
        return pl.ds(pl.multiple_of(row, SUB), self.rows), pl.ds(pl.multiple_of(col, LANE), self.cols)

    def place(self, owner, chunk):
        row = (owner // self.across) * self.rows + chunk * SUB
        col = (owner % self.across) * self.cols
        return pl.ds(pl.multiple_of(row, SUB), SUB), pl.ds(pl.multiple_of(col, LANE), self.cols)


def peer(k):
    return lax.axis_index("sec") ^ k


def cut_kernel(plan, soot, *rest):
    outs, sems = rest[:-1], rest[-1]
    copies = []
    for k in range(plan.n):
        rows, cols = plan.whole(peer(k))
        copies.append(pltpu.make_async_copy(soot.at[:, rows, cols], outs[k], sems.at[k]))
        copies[-1].start()
    for copy in copies:
        copy.wait()


def cut(plan, soot):
    shape = jax.ShapeDtypeStruct((soot.shape[0], plan.rows, plan.cols), F32)
    return pl.pallas_call(
        functools.partial(cut_kernel, plan),
        out_shape=[shape] * plan.n,
        in_specs=[HBM],
        out_specs=[VMEM] * plan.n,
        scratch_shapes=[pltpu.SemaphoreType.DMA((plan.n,))],
        compiler_params=PARAMS,
        name="cut",
    )(pltpu.with_memory_space_constraint(soot, pltpu.HBM))


def edge_kernel(soot, species, after, head, tail):
    local, rows, _ = soot.shape
    for ref, at in ((soot, 0), (species, local)):
        count = ref.shape[0]
        for out, row in ((head, 0), (tail, rows - 1)):
            out[at : at + count, :] = ref[:, row, :]


def edges(soot, species, after):
    shape = jax.ShapeDtypeStruct((soot.shape[0] + species.shape[0], soot.shape[2]), F32)
    return pl.pallas_call(
        edge_kernel,
        out_shape=[shape, shape],
        in_specs=[VMEM, VMEM, ANY],
        out_specs=[VMEM, VMEM],
        compiler_params=PARAMS,
        name="edges",
    )(soot, species, after)


def weight_kernel(kernel, split, target, growth, twice, rest, rate, rate_before, scratch):
    size = kernel.shape[0]
    row = lax.broadcasted_iota(jnp.int32, (size, size), 0)
    col = lax.broadcasted_iota(jnp.int32, (size, size), 1)
    k, sp = kernel[...], split[...]
    t = target[...].astype(F32)
    rowf = row.astype(F32)
    k_t, sp_t, t_t = k.T, sp.T, t.T
    low, high = 0.5 * k * sp, 0.5 * k * (1.0 - sp)
    low_t, high_t = 0.5 * k_t * sp_t, 0.5 * k_t * (1.0 - sp_t)

    def fed(shift):
        at = rowf + shift
        own = jnp.where(t == at, low, 0.0) + jnp.where(t + 1.0 == at, high, 0.0)
        other = jnp.where(t_t == at, low_t, 0.0) + jnp.where(t_t + 1.0 == at, high_t, 0.0)
        return jnp.where(col <= row, own, 0.0) + jnp.where(col < row, other, 0.0)

    scratch[...] = jnp.zeros_like(scratch)
    scratch[0:size, :] = fed(0) - k
    for shift in range(1, SHIFTS):
        scratch[shift * size + shift : (shift + 1) * size, :] = fed(shift)[: size - shift]
    last = SHIFTS * size
    scratch[last : last + SUB - 1, :] = fed(-1)[size - SUB + 1 :]
    w_high, w_low = halves(scratch[...])
    twice[:, :size] = w_high
    twice[:, size:] = w_high
    rest[...] = w_low
    diagonal = jnp.where(row == col, jnp.broadcast_to(growth[...], (size, size)), 0.0)
    column = jnp.sum(diagonal, axis=1, keepdims=True)
    rate[...] = jnp.broadcast_to(column, rate.shape)
    before = jnp.where(row == col + 1, jnp.broadcast_to(growth[...], (size, size)), 0.0)
    column = jnp.sum(before, axis=1, keepdims=True)
    rate_before[...] = jnp.broadcast_to(column, rate_before.shape)


def weights(plan, kernel, split, target, growth):
    size = kernel.shape[0]
    depth = SHIFTS * size + 2 * SUB
    return pl.pallas_call(
        weight_kernel,
        out_shape=[
            jax.ShapeDtypeStruct((depth, 2 * size), BF16),
            jax.ShapeDtypeStruct((depth, size), BF16),
            jax.ShapeDtypeStruct((size, plan.cols), F32),
            jax.ShapeDtypeStruct((size, plan.cols), F32),
        ],
        in_specs=[VMEM] * 4,
        out_specs=[VMEM] * 4,
        scratch_shapes=[pltpu.VMEM((depth, size), F32)],
        compiler_params=PARAMS,
        name="weights",
    )(kernel, split, target, growth.reshape(1, size))


def rate_kernel(plan, chunk, twice, rest, rate, rate_before, acet, after, *refs):
    n = plan.n
    pieces, outs = refs[:n], refs[n : 2 * n]
    whole, result, near, sem = refs[2 * n :]
    size = rate.shape[0]
    local = size // n
    rows, cols = plan.place(lax.axis_index("sec"), chunk)
    copy = pltpu.make_async_copy(acet.at[0, rows, cols], near, sem)
    copy.start()
    pad = SHIFTS - 1
    blocks = range(plan.cols // LANE)
    lanes = [slice(b * LANE, (b + 1) * LANE) for b in blocks]
    for b in blocks:
        whole[b, : pad * SUB, :] = jnp.zeros((pad * SUB, LANE), F32)
        whole[b, (pad + size) * SUB :, :] = jnp.zeros((SUB, LANE), F32)
        for k in range(n):
            start = pl.multiple_of((pad + local * peer(k)) * SUB, SUB)
            piece = pieces[k][:, chunk * SUB : (chunk + 1) * SUB, lanes[b]]
            whole[b, pl.ds(start, local * SUB), :] = piece.reshape(local * SUB, LANE)
    copy.wait()

    def sections(first, count, row):
        parts = [whole[b, pl.ds((pad + first) * SUB + row, count, stride=SUB), :] for b in blocks]
        return jnp.concatenate(parts, axis=1)

    for row in range(SUB):
        here = sections(0, size, row)
        high, low = halves(here)
        product = jnp.dot(twice[...], jnp.concatenate([high, low], axis=0), preferred_element_type=F32)
        product += jnp.dot(rest[...], high, preferred_element_type=F32)
        total = here * product[:size]
        for shift in range(1, SHIFTS):
            total += sections(-shift, size, row) * product[shift * size : (shift + 1) * size]
        last = SHIFTS * size
        extra = sections(size - SUB + 1, SUB, row) * product[last : last + SUB]
        total = jnp.concatenate([total[: size - SUB], total[size - SUB :] + extra], axis=0)
        growing = near[row : row + 1, :]
        grown = rate[...] * here
        total -= growing * (grown - rate_before[...] * sections(-1, size, row))
        for b in blocks:
            result[b, pl.ds(row, size, stride=SUB), :] = total[:, lanes[b]]
        used = growing * jnp.sum(grown, axis=0, keepdims=True)
        for k in range(n):
            outs[k][local * SUB + row : local * SUB + row + 1, :] = used
    for k in range(n):
        start = pl.multiple_of(local * peer(k) * SUB, SUB)
        for b in blocks:
            outs[k][: local * SUB, lanes[b]] = result[b, pl.ds(start, local * SUB), :]


def rates(plan, chunk, prepared, acet, after, pieces):
    size = prepared[2].shape[0]
    local = size // plan.n
    shape = jax.ShapeDtypeStruct(((local + 1) * SUB, plan.cols), F32)
    outs = pl.pallas_call(
        functools.partial(rate_kernel, plan, chunk),
        out_shape=[shape] * plan.n,
        in_specs=[VMEM] * 4 + [ANY] * 2 + [VMEM] * plan.n,
        out_specs=[VMEM] * plan.n,
        scratch_shapes=[
            pltpu.VMEM((plan.cols // LANE, (SHIFTS + size) * SUB, LANE), F32),
            pltpu.VMEM((plan.cols // LANE, size * SUB, LANE), F32),
            pltpu.VMEM((SUB, plan.cols), F32),
            pltpu.SemaphoreType.DMA,
        ],
        compiler_params=PARAMS,
        name="rates",
    )(*prepared, acet, after, *pieces)
    return outs


def mix_kernel(reaction, species, mixed, stack):
    kinds, rows, width = species.shape
    blocks = range(width // LANE)
    for b in blocks:
        stack[b] = species[:, :, b * LANE : (b + 1) * LANE].reshape(kinds * rows, LANE)
    r_high, r_low = halves(reaction[...])
    r_all = jnp.concatenate([r_high.astype(F32), r_high.astype(F32), r_low.astype(F32)], axis=1).astype(BF16)
    for row in range(rows):
        at = pl.ds(row, kinds, stride=rows)
        v = jnp.concatenate([stack[b, at, :] for b in blocks], axis=1)
        high, low = halves(v)
        high, low = high.astype(F32), low.astype(F32)
        v_all = jnp.concatenate([high, low, high], axis=0).astype(BF16)
        product = jnp.dot(r_all, v_all, preferred_element_type=F32)
        for b in blocks:
            mixed[b, at, :] = product[:, b * LANE : (b + 1) * LANE]


def mix(reaction, species):
    shape = (species.shape[2] // LANE, species.shape[0] * species.shape[1], LANE)
    return pl.pallas_call(
        mix_kernel,
        out_shape=jax.ShapeDtypeStruct(shape, F32),
        in_specs=[VMEM, VMEM],
        out_specs=VMEM,
        scratch_shapes=[pltpu.VMEM(shape, F32)],
        compiler_params=PARAMS,
        name="mix",
    )(reaction, species)


def base_kernel(above, below, diffusivity, mixed, soot, species, after, soot_base, species_base):
    local, rows, width = soot.shape
    kinds = species.shape[0]
    lanes = lax.broadcasted_iota(jnp.int32, (rows, width), 1)
    blocks = range(width // LANE)

    def spread(v, at, factor):
        up = jnp.concatenate([above[pl.ds(at, 1), :], v[:-1]], axis=0)
        down = jnp.concatenate([v[1:], below[pl.ds(at, 1), :]], axis=0)
        left = jnp.where(lanes == 0, 0.0, pltpu.roll(v, 1, 1))
        right = jnp.where(lanes == width - 1, 0.0, pltpu.roll(v, width - 1, 1))
        return v + factor * (up + down + left + right - 4.0 * v)

    def one_section(i, carry):
        soot_base[i] = spread(soot[i], i, 0.1)
        return carry

    lax.fori_loop(0, local, one_section, 0, unroll=2)

    def one_species(i, carry):
        at = pl.ds(pl.multiple_of(i * rows, SUB), rows)
        more = jnp.concatenate([mixed[b, at, :] for b in blocks], axis=1)
        species_base[i] = spread(species[i], local + i, diffusivity[i]) + more
        return carry

    lax.fori_loop(0, kinds, one_species, 0, unroll=2)


def bases(above, below, diffusivity, mixed, soot, species, after):
    return pl.pallas_call(
        base_kernel,
        out_shape=[jax.ShapeDtypeStruct(soot.shape, F32), jax.ShapeDtypeStruct(species.shape, F32)],
        in_specs=[VMEM, VMEM, SMEM, VMEM, VMEM, VMEM, ANY],
        out_specs=[VMEM, VMEM],
        compiler_params=PARAMS,
        name="bases",
    )(above, below, diffusivity, mixed, soot, species, after)


def last_kernel(plan, chunk, stoich, soot_base, species_base, *refs):
    n = plan.n
    pieces, refs = refs[:n], refs[n:]
    soot_out, species_out, soot_held, species_held, sems = refs[-5:]
    local, kinds = soot_out.shape[0], species_out.shape[0]
    copies = []
    for k in range(n):
        rows, cols = plan.place(peer(k), chunk)
        soot_held[k] = soot_base[:, rows, cols] + pieces[k][:local]
        copies.append(pltpu.make_async_copy(soot_held.at[k], soot_out.at[:, rows, cols], sems.at[0, k]))
        copies[-1].start()
        used = pieces[k][local]
        for kind in range(kinds):
            species_held[k, kind] = species_base[kind, rows, cols] - stoich[kind] * used
        copies.append(pltpu.make_async_copy(species_held.at[k], species_out.at[:, rows, cols], sems.at[1, k]))
        copies[-1].start()
    for copy in copies:
        copy.wait()


def last(plan, chunk, stoich, soot_base, species_base, pieces, before):
    local, kinds = soot_base.shape[0], species_base.shape[0]
    first = 3 + len(pieces)
    return pl.pallas_call(
        functools.partial(last_kernel, plan, chunk),
        out_shape=[jax.ShapeDtypeStruct(soot_base.shape, F32), jax.ShapeDtypeStruct(species_base.shape, F32)],
        in_specs=[SMEM, VMEM, VMEM] + [VMEM] * len(pieces) + [HBM] * len(before),
        out_specs=[HBM, HBM],
        scratch_shapes=[
            pltpu.VMEM((plan.n, local, SUB, plan.cols), F32),
            pltpu.VMEM((plan.n, kinds, SUB, plan.cols), F32),
            pltpu.SemaphoreType.DMA((2, plan.n)),
        ],
        input_output_aliases={first + i: i for i in range(len(before))},
        compiler_params=PARAMS,
        name="last",
    )(stoich, soot_base, species_base, *[p.reshape(local + 1, SUB, plan.cols) for p in pieces], *before)


def shards(soot, species, kernel, split, target, growth, diffusivity, reaction, stoich):
    n = lax.axis_size("sec")
    plan = Plan(n, soot.shape[1], soot.shape[2])

    def swap(x, k):
        return lax.ppermute(x, "sec", [(i, i ^ k) for i in range(n)]) if k else x

    sent = cut(plan, soot)
    got = [swap(sent[k], k) for k in range(n)]
    prepared = weights(plan, kernel, split, target, growth)
    mixed = mix(reaction, species)
    head, tail = edges(soot, species, sent[0])
    count = lax.axis_size("xs")
    above = lax.ppermute(tail, "xs", [(i, i + 1) for i in range(count - 1)])
    below = lax.ppermute(head, "xs", [(i + 1, i) for i in range(count - 1)])
    soot_base, species_base = bases(above, below, diffusivity, mixed, soot, species, mixed)
    back = []
    for chunk in range(plan.chunks):
        outs = rates(plan, chunk, prepared, species, soot_base, got)
        back.append([swap(outs[k], k) for k in range(n)])
    result = ()
    for chunk in range(plan.chunks):
        result = last(plan, chunk, stoich, soot_base, species_base, back[chunk], result)
    return tuple(result)


def solution(mesh):
    return jax.shard_map(
        shards,
        mesh=mesh,
        in_specs=(P("sec", "xs", None), P(None, "xs", None), P(), P(), P(), P(), P(), P(), P()),
        out_specs=(P("sec", "xs", None), P(None, "xs", None)),
        check_vma=False,
    )
```

```python
import functools

import jax
import jax.numpy as jnp
from jax import lax
from jax.experimental import pallas as pl
from jax.experimental.pallas import tpu as pltpu
from jax.sharding import PartitionSpec as P

F32 = jnp.float32
BF16 = jnp.bfloat16
SUB = 8
LANE = 128
GROUP = 2
SHIFTS = 5
ANY = pl.BlockSpec(memory_space=pl.ANY)
VMEM = pl.BlockSpec(memory_space=pltpu.VMEM)
SMEM = pl.BlockSpec(memory_space=pltpu.SMEM)
HBM = pl.BlockSpec(memory_space=pltpu.HBM)
PARAMS = pltpu.CompilerParams(vmem_limit_bytes=16 * 1024 * 1024)


def halves(x):
    high = x.astype(BF16)
    return high, (x - high.astype(F32)).astype(BF16)


class Plan:
    def __init__(self, n, rows, width):
        self.n = n
        self.across = min(n, width // LANE)
        self.rows = rows // (n // self.across)
        self.cols = width // self.across
        self.blocks = [(r, c) for r in range(self.rows // SUB) for c in range(self.cols // LANE)]

    def parts(self, ends):
        stops = [round(end * len(self.blocks)) for end in ends]
        whole = list(range(len(self.blocks)))
        return [p for p in (whole[x:y] for x, y in zip([0] + stops, stops + [None])) if p]

    def place(self, owner, block):
        r, c = self.blocks[block]
        row = (owner // self.across) * self.rows + r * SUB
        col = (owner % self.across) * self.cols + c * LANE
        return pl.ds(pl.multiple_of(row, SUB), SUB), pl.ds(pl.multiple_of(col, LANE), LANE)


def peer(k):
    return lax.axis_index("sec") ^ k


def cut_kernel(plan, pieces, soot, *rest):
    outs, sem = rest[:-1], rest[-1]
    copies = []
    for out, (k, part) in zip(outs, pieces):
        for b, block in enumerate(part):
            rows, cols = plan.place(peer(k), block)
            copies.append(pltpu.make_async_copy(soot.at[:, rows, cols], out.at[b], sem.at[len(copies)]))
            copies[-1].start()
    for copy in copies:
        copy.wait()


def cut(plan, pieces, soot):
    shapes = [jax.ShapeDtypeStruct((len(part), soot.shape[0], SUB, LANE), F32) for _, part in pieces]
    return pl.pallas_call(
        functools.partial(cut_kernel, plan, pieces),
        out_shape=shapes,
        in_specs=[HBM],
        out_specs=[VMEM] * len(shapes),
        scratch_shapes=[pltpu.SemaphoreType.DMA((sum(len(part) for _, part in pieces),))],
        compiler_params=PARAMS,
        name="cut",
    )(pltpu.with_memory_space_constraint(soot, pltpu.HBM))


def edge_kernel(soot, species, after, inner, outer):
    local, rows, _ = soot.shape
    odd = lax.axis_index("xs") % 2 == 1
    for ref, at in ((soot, 0), (species, local)):
        count = ref.shape[0]
        head, tail = ref[:, 0, :], ref[:, rows - 1, :]
        inner[at : at + count, :] = jnp.where(odd, head, tail)
        outer[at : at + count, :] = jnp.where(odd, tail, head)


def edges(soot, species, after):
    shape = jax.ShapeDtypeStruct((soot.shape[0] + species.shape[0], soot.shape[2]), F32)
    return pl.pallas_call(
        edge_kernel,
        out_shape=[shape, shape],
        in_specs=[VMEM, VMEM, ANY],
        out_specs=[VMEM, VMEM],
        compiler_params=PARAMS,
        name="edges",
    )(soot, species, after)


def weight_kernel(kernel, split, target, growth, reaction, stack, rate, rate_before, spread_out, scratch):
    size = kernel.shape[0]
    row = lax.broadcasted_iota(jnp.int32, (size, size), 0)
    col = lax.broadcasted_iota(jnp.int32, (size, size), 1)
    k, sp = kernel[...], split[...]
    t = target[...].astype(F32)
    rowf = row.astype(F32)
    k_t, sp_t, t_t = k.T, sp.T, t.T
    low, high = 0.5 * k * sp, 0.5 * k * (1.0 - sp)
    low_t, high_t = 0.5 * k_t * sp_t, 0.5 * k_t * (1.0 - sp_t)

    def fed(shift):
        at = rowf + shift
        own = jnp.where(t == at, low, 0.0) + jnp.where(t + 1.0 == at, high, 0.0)
        other = jnp.where(t_t == at, low_t, 0.0) + jnp.where(t_t + 1.0 == at, high_t, 0.0)
        return jnp.where(col <= row, own, 0.0) + jnp.where(col < row, other, 0.0)

    scratch[...] = jnp.zeros_like(scratch)
    scratch[0:size, :] = fed(0) - k
    for shift in range(1, SHIFTS):
        scratch[shift * size + shift : (shift + 1) * size, :] = fed(shift)[: size - shift]
    last = SHIFTS * size
    scratch[last : last + SUB - 1, :] = fed(-1)[size - SUB + 1 :]
    w_high, w_low = halves(scratch[...])
    stack[:, :size] = w_high
    stack[:, size : 2 * size] = w_high
    stack[:, 2 * size :] = w_low
    diagonal = jnp.where(row == col, jnp.broadcast_to(growth[...], (size, size)), 0.0)
    column = jnp.sum(diagonal, axis=1, keepdims=True)
    rate[...] = jnp.broadcast_to(column, rate.shape)
    before = jnp.where(row == col + 1, jnp.broadcast_to(growth[...], (size, size)), 0.0)
    column = jnp.sum(before, axis=1, keepdims=True)
    rate_before[...] = jnp.broadcast_to(column, rate_before.shape)


    kinds = reaction.shape[0]
    wide = kinds * SUB
    tall = lax.broadcasted_iota(jnp.int32, (wide, kinds), 0) // SUB == lax.broadcasted_iota(jnp.int32, (wide, kinds), 1)
    flat = lax.broadcasted_iota(jnp.int32, (kinds, wide), 1) // SUB == lax.broadcasted_iota(jnp.int32, (kinds, wide), 0)
    tall, flat = tall.astype(F32).astype(BF16), flat.astype(F32).astype(BF16)
    same = lax.broadcasted_iota(jnp.int32, (wide, wide), 0) % SUB == lax.broadcasted_iota(jnp.int32, (wide, wide), 1) % SUB
    wider = []
    for half in halves(reaction[...]):
        rows = jnp.dot(tall, half, preferred_element_type=F32).astype(BF16)
        wider.append(jnp.where(same, jnp.dot(rows, flat, preferred_element_type=F32), 0.0))
    spread_out[...] = jnp.concatenate([wider[0], wider[0], wider[1]], axis=1).astype(BF16)


def weights(plan, kernel, split, target, growth, reaction):
    size, kinds = kernel.shape[0], reaction.shape[0]
    depth = SHIFTS * size + 2 * SUB
    return pl.pallas_call(
        weight_kernel,
        out_shape=[
            jax.ShapeDtypeStruct((depth, 3 * size), BF16),
            jax.ShapeDtypeStruct((size, GROUP * LANE), F32),
            jax.ShapeDtypeStruct((size, GROUP * LANE), F32),
            jax.ShapeDtypeStruct((kinds * SUB, 3 * kinds * SUB), BF16),
        ],
        in_specs=[VMEM] * 5,
        out_specs=[VMEM] * 4,
        scratch_shapes=[pltpu.VMEM((depth, size), F32)],
        compiler_params=PARAMS,
        name="weights",
    )(kernel, split, target, growth.reshape(1, size), reaction)


def rate_kernel(plan, sources, count, part, stack, rate, rate_before, soot, acet, after, *refs):
    n = plan.n
    pieces, outs = refs[:count], refs[count : count + n]
    whole, result, near, shifted = refs[count + n :]
    size = rate.shape[0]
    local = size // n
    for b, block in enumerate(part):
        rows, cols = plan.place(lax.axis_index("sec"), block)
        near[b] = acet[0, rows, cols]
    pad = SHIFTS - 1
    for b in range(len(part)):
        whole[b, : pad * SUB, :] = jnp.zeros((pad * SUB, LANE), F32)
        whole[b, (pad + size) * SUB :, :] = jnp.zeros((SUB, LANE), F32)
        for k in range(n):
            start = pl.multiple_of((pad + local * peer(k)) * SUB, SUB)
            if k:
                source, at = sources[k, b]
                piece = pieces[source][at]
            else:
                rows, cols = plan.place(lax.axis_index("sec"), part[b])
                piece = soot[:, rows, cols]
            whole[b, pl.ds(start, local * SUB), :] = piece.reshape(local * SUB, LANE)
    def sections(first, count, pair):
        found = [whole[b, pl.ds((pad + first) * SUB + row, count, stride=SUB), :] for b, row in pair]
        return jnp.concatenate(found, axis=1)

    units = [(b, row) for row in range(SUB) for b in range(len(part))]
    for i in range(GROUP):
        shifted[:, i, :pad, :] = jnp.zeros((2, pad, LANE), F32)
        shifted[:, i, pad + size :, :] = jnp.zeros((2, SHIFTS + SUB - pad, LANE), F32)
    for step, pair in enumerate([units[i : i + GROUP] for i in range(0, len(units), GROUP)]):
        here = sections(0, size, pair)
        moved = shifted.at[step % 2]
        for i in range(GROUP):
            moved[i, pad : pad + size, :] = here[:, i * LANE : (i + 1) * LANE]

        def near_by(first, count):
            return jnp.concatenate([moved[i, pad + first : pad + first + count, :] for i in range(GROUP)], axis=1)

        high, low = halves(here)
        product = jnp.dot(stack[...], jnp.concatenate([high, low, high], axis=0), preferred_element_type=F32)
        total = here * product[:size]
        for shift in range(1, SHIFTS):
            total += near_by(-shift, size) * product[shift * size : (shift + 1) * size]
        last = SHIFTS * size
        extra = near_by(size - SUB + 1, SUB) * product[last : last + SUB]
        total = jnp.concatenate([total[: size - SUB], total[size - SUB :] + extra], axis=0)
        growing = jnp.concatenate([near[b, row : row + 1, :] for b, row in pair], axis=1)
        grown = rate[...] * here
        total -= growing * (grown - rate_before[...] * near_by(-1, size))
        used = growing * jnp.sum(grown, axis=0, keepdims=True)
        for i, (b, row) in enumerate(pair):
            lanes = slice(i * LANE, (i + 1) * LANE)
            result[b, pl.ds(row, size, stride=SUB), :] = total[:, lanes]
            for k in range(n):
                outs[k][b, local, row : row + 1, :] = used[:, lanes]
    for b in range(len(part)):
        for k in range(n):
            start = pl.multiple_of(local * peer(k) * SUB, SUB)
            outs[k][b, :local] = result[b, pl.ds(start, local * SUB), :].reshape(local, SUB, LANE)


def rates(plan, part, prepared, soot, acet, after, pieces, got):
    size = prepared[1].shape[0]
    local = size // plan.n
    sources, used = {}, []
    for (k, blocks), x in zip(pieces, got):
        if set(blocks) & set(part):
            for block in set(blocks) & set(part):
                sources[k, part.index(block)] = (len(used), blocks.index(block))
            used.append(x)
    shape = jax.ShapeDtypeStruct((len(part), local + 1, SUB, LANE), F32)
    return pl.pallas_call(
        functools.partial(rate_kernel, plan, sources, len(used), part),
        out_shape=[shape] * plan.n,
        in_specs=[VMEM] * 5 + [ANY] + [VMEM] * len(used),
        out_specs=[VMEM] * plan.n,
        scratch_shapes=[
            pltpu.VMEM((len(part), (SHIFTS + size) * SUB, LANE), F32),
            pltpu.VMEM((len(part), size * SUB, LANE), F32),
            pltpu.VMEM((len(part), SUB, LANE), F32),
            pltpu.VMEM((2, GROUP, SHIFTS + SUB + size, LANE), F32),
        ],
        compiler_params=PARAMS,
        name="rates",
    )(*prepared, soot, acet, after, *used)


def gate(pieces, late):
    return pl.pallas_call(
        lambda *refs: None,
        out_shape=[jax.ShapeDtypeStruct(x.shape, x.dtype) for x in pieces],
        in_specs=[VMEM] * len(pieces) + [ANY] * len(late),
        out_specs=[VMEM] * len(pieces),
        input_output_aliases={i: i for i in range(len(pieces))},
        compiler_params=PARAMS,
        name="gate",
    )(*pieces, *late)


def base_kernel(diffusivity, kinetics, soot, species, soot_base, species_base):
    local, rows, width = soot.shape
    kinds = species.shape[0]
    lanes = lax.broadcasted_iota(jnp.int32, (rows, LANE), 1)
    none = jnp.zeros((1, width), F32)

    def spread(v, factor):
        up = jnp.concatenate([none, v[:-1]], axis=0)
        down = jnp.concatenate([v[1:], none], axis=0)
        left, right = pltpu.roll(v, 1, 1), pltpu.roll(v, width - 1, 1)
        left = jnp.concatenate([jnp.where(lanes == 0, 0.0, left[:, :LANE]), left[:, LANE:]], axis=1)
        right = jnp.concatenate([right[:, :-LANE], jnp.where(lanes == LANE - 1, 0.0, right[:, -LANE:])], axis=1)
        return (1.0 - 4.0 * factor) * v + factor * ((up + down) + (left + right))

    def one_section(i, carry):
        soot_base[i] = spread(soot[i], 0.1)
        return carry

    lax.fori_loop(0, local, one_section, 0, unroll=8)

    for row in range(0, rows, SUB):
        for col in range(0, width, 2 * LANE):
            tile = (slice(None), slice(row, row + SUB), slice(col, col + 2 * LANE))
            high, low = halves(species[tile].reshape(kinds * SUB, 2 * LANE))
            product = jnp.dot(kinetics[...], jnp.concatenate([high, low, high], axis=0), preferred_element_type=F32)
            species_base[tile] = product.reshape(kinds, SUB, 2 * LANE)

    def one_species(i, carry):
        species_base[i] += spread(species[i], diffusivity[i])
        return carry

    lax.fori_loop(0, kinds, one_species, 0, unroll=8)


def bases(diffusivity, kinetics, soot, species):
    return pl.pallas_call(
        base_kernel,
        out_shape=[jax.ShapeDtypeStruct(soot.shape, F32), jax.ShapeDtypeStruct(species.shape, F32)],
        in_specs=[SMEM, VMEM, VMEM, VMEM],
        out_specs=[VMEM, VMEM],
        compiler_params=PARAMS,
        name="bases",
    )(diffusivity, kinetics, soot, species)


def rim_kernel(inner, outer, diffusivity, soot_in, species_in, soot_base, species_base):
    local, rows, _ = soot_base.shape
    odd = lax.axis_index("xs") % 2 == 1
    for ref, at in ((soot_base, 0), (species_base, local)):
        for i in range(ref.shape[0]):
            factor = diffusivity[i] if at else 0.1
            one, other = inner[at + i : at + i + 1, :], outer[at + i : at + i + 1, :]
            ref[i, 0:1, :] += factor * jnp.where(odd, one, other)
            ref[i, rows - 1 : rows, :] += factor * jnp.where(odd, other, one)


def rim(inner, outer, diffusivity, soot_base, species_base):
    return pl.pallas_call(
        rim_kernel,
        out_shape=[jax.ShapeDtypeStruct(soot_base.shape, F32), jax.ShapeDtypeStruct(species_base.shape, F32)],
        in_specs=[VMEM, VMEM, SMEM, VMEM, VMEM],
        out_specs=[VMEM, VMEM],
        input_output_aliases={3: 0, 4: 1},
        compiler_params=PARAMS,
        name="rim",
    )(inner, outer, diffusivity, soot_base, species_base)


def last_kernel(plan, part, peers, stoich, soot_base, species_base, *refs):
    pieces = refs[: len(peers)]
    soot_out, species_out, soot_held, species_held, sems = refs[-5:]
    local, kinds = soot_out.shape[0], species_out.shape[0]
    copies = []
    for k, far in enumerate(peers):
        for b, block in enumerate(part):
            rows, cols = plan.place(peer(far), block)
            soot_held[k, b] = soot_base[:, rows, cols] + pieces[k][b, :local]
            copies.append(pltpu.make_async_copy(soot_held.at[k, b], soot_out.at[:, rows, cols], sems.at[0, k, b]))
            copies[-1].start()
            used = pieces[k][b, local]
            for kind in range(kinds):
                species_held[k, b, kind] = species_base[kind, rows, cols] - stoich[kind] * used
            copies.append(pltpu.make_async_copy(species_held.at[k, b], species_out.at[:, rows, cols], sems.at[1, k, b]))
            copies[-1].start()
    for copy in copies:
        copy.wait()


def last(plan, part, peers, stoich, soot_base, species_base, pieces, before):
    local, kinds = soot_base.shape[0], species_base.shape[0]
    first = 3 + len(pieces)
    return pl.pallas_call(
        functools.partial(last_kernel, plan, part, peers),
        out_shape=[jax.ShapeDtypeStruct(soot_base.shape, F32), jax.ShapeDtypeStruct(species_base.shape, F32)],
        in_specs=[SMEM, VMEM, VMEM] + [VMEM] * len(pieces) + [HBM] * len(before),
        out_specs=[HBM, HBM],
        scratch_shapes=[
            pltpu.VMEM((len(peers), len(part), local, SUB, LANE), F32),
            pltpu.VMEM((len(peers), len(part), kinds, SUB, LANE), F32),
            pltpu.SemaphoreType.DMA((2, len(peers), len(part))),
        ],
        input_output_aliases={first + i: i for i in range(len(before))},
        compiler_params=PARAMS,
        name="last",
    )(stoich, soot_base, species_base, *pieces, *before)


def shards(soot, species, kernel, split, target, growth, diffusivity, reaction, stoich):
    n = lax.axis_size("sec")
    count = lax.axis_size("xs")
    plan = Plan(n, soot.shape[1], soot.shape[2])

    def swap(x, k):
        return lax.ppermute(x, "sec", [(i, i ^ k) for i in range(n)])

    order = [k for k in (2, 1, 3) if k < n] + list(range(4, n))
    pieces = [(k, part) for k in order for part in plan.parts((0.75,) if k == n - 1 else ())]
    sent = cut(plan, pieces, soot)
    got = [swap(x, k) for (k, _), x in zip(pieces, sent)]

    inner, outer = edges(soot, species, sent[0])
    pairs = [[(i, i + 1) for i in range(first, count - 1, 2)] for first in (0, 1)]
    inner, outer = (lax.ppermute(x, "xs", [q for i, j in p for q in ((i, j), (j, i))]) for x, p in zip((inner, outer), pairs))
    *prepared, kinetics = weights(plan, kernel, split, target, growth, reaction)
    base = bases(diffusivity, kinetics, soot, species)
    base = rim(inner, outer, diffusivity, *base)

    back = []
    for part in plan.parts((0.5,)):
        outs = rates(plan, part, prepared, soot, species, base[0] if not back else stoich, pieces, got)
        late = [x for (_, blocks), x in zip(pieces, got) if not set(blocks) & set(part)]
        away = gate(outs[1:], late) if late else outs[1:]
        back.append((part, [outs[0]] + [swap(x, k) for k, x in enumerate(away, 1)]))
    result = ()
    for i, (part, moved) in enumerate(back):
        early = 2 if i == len(back) - 1 else n
        for peers in (range(early), range(early, n)):
            if peers:
                result = last(plan, part, peers, stoich, *base, [moved[k] for k in peers], result)
    return tuple(result)


def solution(mesh):
    return jax.shard_map(
        shards,
        mesh=mesh,
        in_specs=(P("sec", "xs", None), P(None, "xs", None), P(), P(), P(), P(), P(), P(), P()),
        out_specs=(P("sec", "xs", None), P(None, "xs", None)),
        check_vma=False,
    )
```

```python
import functools

import jax
import jax.numpy as jnp
from jax import lax
from jax.experimental import pallas as pl
from jax.experimental.pallas import tpu as pltpu
from jax.sharding import PartitionSpec as P

F32 = jnp.float32
BF16 = jnp.bfloat16
SUB = 8
LANE = 128
GROUP = 2
SHIFTS = 5
ANY = pl.BlockSpec(memory_space=pl.ANY)
VMEM = pl.BlockSpec(memory_space=pltpu.VMEM)
SMEM = pl.BlockSpec(memory_space=pltpu.SMEM)
HBM = pl.BlockSpec(memory_space=pltpu.HBM)
PARAMS = pltpu.CompilerParams(vmem_limit_bytes=16 * 1024 * 1024)


def halves(x):
    high = x.astype(BF16)
    return high, (x - high.astype(F32)).astype(BF16)


class Plan:
    def __init__(self, n, rows, width):
        self.n = n
        self.across = min(n, width // LANE)
        self.rows = rows // (n // self.across)
        self.cols = width // self.across
        self.blocks = [(r, c) for r in range(self.rows // SUB) for c in range(self.cols // LANE)]

    def parts(self, ends):
        stops = [round(end * len(self.blocks)) for end in ends]
        whole = list(range(len(self.blocks)))
        return [p for p in (whole[x:y] for x, y in zip([0] + stops, stops + [None])) if p]

    def place(self, owner, block):
        r, c = self.blocks[block]
        row = (owner // self.across) * self.rows + r * SUB
        col = (owner % self.across) * self.cols + c * LANE
        return pl.ds(pl.multiple_of(row, SUB), SUB), pl.ds(pl.multiple_of(col, LANE), LANE)


def peer(k):
    return lax.axis_index("sec") ^ k


def cut_kernel(plan, pieces, soot, *rest):
    outs, sem = rest[:-1], rest[-1]
    copies = []
    for out, (k, part) in zip(outs, pieces):
        for b, block in enumerate(part):
            rows, cols = plan.place(peer(k), block)
            copies.append(pltpu.make_async_copy(soot.at[:, rows, cols], out.at[b], sem.at[len(copies)]))
            copies[-1].start()
    for copy in copies:
        copy.wait()


def cut(plan, pieces, soot):
    shapes = [jax.ShapeDtypeStruct((len(part), soot.shape[0], SUB, LANE), F32) for _, part in pieces]
    return pl.pallas_call(
        functools.partial(cut_kernel, plan, pieces),
        out_shape=shapes,
        in_specs=[HBM],
        out_specs=[VMEM] * len(shapes),
        scratch_shapes=[pltpu.SemaphoreType.DMA((sum(len(part) for _, part in pieces),))],
        compiler_params=PARAMS,
        name="cut",
    )(pltpu.with_memory_space_constraint(soot, pltpu.HBM))


def edge_kernel(soot, species, after, inner, outer):
    local, rows, _ = soot.shape
    odd = lax.axis_index("xs") % 2 == 1
    for ref, at in ((soot, 0), (species, local)):
        count = ref.shape[0]
        head, tail = ref[:, 0, :], ref[:, rows - 1, :]
        inner[at : at + count, :] = jnp.where(odd, head, tail)
        outer[at : at + count, :] = jnp.where(odd, tail, head)


def edges(soot, species, after):
    shape = jax.ShapeDtypeStruct((soot.shape[0] + species.shape[0], soot.shape[2]), F32)
    return pl.pallas_call(
        edge_kernel,
        out_shape=[shape, shape],
        in_specs=[VMEM, VMEM, ANY],
        out_specs=[VMEM, VMEM],
        compiler_params=PARAMS,
        name="edges",
    )(soot, species, after)


def weight_kernel(kernel, split, target, growth, reaction, lower, upper, rate, rate_before, spread_out, scratch):
    size = kernel.shape[0]
    row = lax.broadcasted_iota(jnp.int32, (size, size), 0)
    col = lax.broadcasted_iota(jnp.int32, (size, size), 1)
    k, sp = kernel[...], split[...]
    t = target[...].astype(F32)
    rowf = row.astype(F32)
    k_t, sp_t, t_t = k.T, sp.T, t.T
    low, high = 0.5 * k * sp, 0.5 * k * (1.0 - sp)
    low_t, high_t = 0.5 * k_t * sp_t, 0.5 * k_t * (1.0 - sp_t)

    def fed(shift):
        at = rowf + shift
        own = jnp.where(t == at, low, 0.0) + jnp.where(t + 1.0 == at, high, 0.0)
        other = jnp.where(t_t == at, low_t, 0.0) + jnp.where(t_t + 1.0 == at, high_t, 0.0)
        return jnp.where(col <= row, own, 0.0) + jnp.where(col < row, other, 0.0)

    scratch[...] = jnp.zeros_like(scratch)
    scratch[0:size, :] = fed(0) - k
    for shift in range(1, SHIFTS):
        scratch[shift * size + shift : (shift + 1) * size, :] = fed(shift)[: size - shift]
    last = SHIFTS * size
    scratch[last : last + SUB - 1, :] = fed(-1)[size - SUB + 1 :]
    w_high, w_low = halves(scratch[...])
    most = size - 2 * SUB
    for i in range(1, SHIFTS):
        at = slice(most * (i - 1), most * i)
        for j, part in enumerate((w_high, w_high, w_low)):
            lower[at, most * j : most * (j + 1)] = part[i * size : i * size + most, :most]
    rest = [slice(0, size)] + [slice(i * size + most, (i + 1) * size) for i in range(1, SHIFTS)] + [slice(last, last + 2 * SUB)]
    at = 0
    for rows in rest:
        count = rows.stop - rows.start
        for j, part in enumerate((w_high, w_high, w_low)):
            upper[at : at + count, size * j : size * (j + 1)] = part[rows]
        at += count
    diagonal = jnp.where(row == col, jnp.broadcast_to(growth[...], (size, size)), 0.0)
    column = jnp.sum(diagonal, axis=1, keepdims=True)
    rate[...] = jnp.broadcast_to(column, rate.shape)
    before = jnp.where(row == col + 1, jnp.broadcast_to(growth[...], (size, size)), 0.0)
    column = jnp.sum(before, axis=1, keepdims=True)
    rate_before[...] = jnp.broadcast_to(column, rate_before.shape)


    kinds = reaction.shape[0]
    wide = kinds * SUB
    tall = lax.broadcasted_iota(jnp.int32, (wide, kinds), 0) // SUB == lax.broadcasted_iota(jnp.int32, (wide, kinds), 1)
    flat = lax.broadcasted_iota(jnp.int32, (kinds, wide), 1) // SUB == lax.broadcasted_iota(jnp.int32, (kinds, wide), 0)
    tall, flat = tall.astype(F32).astype(BF16), flat.astype(F32).astype(BF16)
    same = lax.broadcasted_iota(jnp.int32, (wide, wide), 0) % SUB == lax.broadcasted_iota(jnp.int32, (wide, wide), 1) % SUB
    wider = []
    for half in halves(reaction[...]):
        rows = jnp.dot(tall, half, preferred_element_type=F32).astype(BF16)
        wider.append(jnp.where(same, jnp.dot(rows, flat, preferred_element_type=F32), 0.0))
    spread_out[...] = jnp.concatenate([wider[0], wider[0], wider[1]], axis=1).astype(BF16)


def weights(plan, kernel, split, target, growth, reaction):
    size, kinds = kernel.shape[0], reaction.shape[0]
    depth = SHIFTS * size + 2 * SUB
    return pl.pallas_call(
        weight_kernel,
        out_shape=[
            jax.ShapeDtypeStruct(((SHIFTS - 1) * (size - 2 * SUB), 3 * (size - 2 * SUB)), BF16),
            jax.ShapeDtypeStruct((size + 2 * SUB * SHIFTS, 3 * size), BF16),
            jax.ShapeDtypeStruct((size, GROUP * LANE), F32),
            jax.ShapeDtypeStruct((size, GROUP * LANE), F32),
            jax.ShapeDtypeStruct((kinds * SUB, 3 * kinds * SUB), BF16),
        ],
        in_specs=[VMEM] * 5,
        out_specs=[VMEM] * 5,
        scratch_shapes=[pltpu.VMEM((depth, size), F32)],
        compiler_params=PARAMS,
        name="weights",
    )(kernel, split, target, growth.reshape(1, size), reaction)


def rate_kernel(plan, sources, count, part, lower, upper, rate, rate_before, soot, acet, after, *refs):
    n = plan.n
    pieces, outs = refs[:count], refs[count : count + n]
    whole, result, near, shifted = refs[count + n :]
    size = rate.shape[0]
    local = size // n
    for b, block in enumerate(part):
        rows, cols = plan.place(lax.axis_index("sec"), block)
        near[b] = acet[0, rows, cols]
    pad, most = SHIFTS - 1, size - 2 * SUB
    for b in range(len(part)):
        whole[b, : pad * SUB, :] = jnp.zeros((pad * SUB, LANE), F32)
        whole[b, (pad + size) * SUB :, :] = jnp.zeros((SUB, LANE), F32)
        for k in range(n):
            start = pl.multiple_of((pad + local * peer(k)) * SUB, SUB)
            if k:
                source, at = sources[k, b]
                piece = pieces[source][at]
            else:
                rows, cols = plan.place(lax.axis_index("sec"), part[b])
                piece = soot[:, rows, cols]
            whole[b, pl.ds(start, local * SUB), :] = piece.reshape(local * SUB, LANE)
    def sections(first, count, pair):
        found = [whole[b, pl.ds((pad + first) * SUB + row, count, stride=SUB), :] for b, row in pair]
        return jnp.concatenate(found, axis=1)

    units = [(b, row) for row in range(SUB) for b in range(len(part))]
    for i in range(GROUP):
        shifted[:, i, :pad, :] = jnp.zeros((2, pad, LANE), F32)
        shifted[:, i, pad + size :, :] = jnp.zeros((2, SHIFTS + SUB - pad, LANE), F32)
    for step, pair in enumerate([units[i : i + GROUP] for i in range(0, len(units), GROUP)]):
        here = sections(0, size, pair)
        moved = shifted.at[step % 2]
        for i in range(GROUP):
            moved[i, pad : pad + size, :] = here[:, i * LANE : (i + 1) * LANE]

        def near_by(first, count):
            return jnp.concatenate([moved[i, pad + first : pad + first + count, :] for i in range(GROUP)], axis=1)

        high, low = halves(here)
        product = jnp.dot(upper[...], jnp.concatenate([high, low, high], axis=0), preferred_element_type=F32)
        high, low = high[:most], low[:most]
        below = jnp.dot(lower[...], jnp.concatenate([high, low, high], axis=0), preferred_element_type=F32)
        total = here * product[:size]
        for shift in range(1, SHIFTS):
            moved_here = near_by(-shift, size)
            before = moved_here if shift == 1 else before
            top = size + 2 * SUB * (shift - 1)
            total += moved_here * jnp.concatenate([below[most * (shift - 1) : most * shift], product[top : top + 2 * SUB]], axis=0)
        last = size + 2 * SUB * (SHIFTS - 1)
        extra = near_by(size - SUB + 1, SUB) * product[last : last + SUB]
        total = jnp.concatenate([total[: size - SUB], total[size - SUB :] + extra], axis=0)
        growing = jnp.concatenate([near[b, row : row + 1, :] for b, row in pair], axis=1)
        grown = rate[...] * here
        total -= growing * (grown - rate_before[...] * before)
        used = growing * jnp.sum(grown, axis=0, keepdims=True)
        for i, (b, row) in enumerate(pair):
            lanes = slice(i * LANE, (i + 1) * LANE)
            result[b, pl.ds(row, size, stride=SUB), :] = total[:, lanes]
            for k in range(n):
                outs[k][b, local, row : row + 1, :] = used[:, lanes]
    for b in range(len(part)):
        for k in range(n):
            start = pl.multiple_of(local * peer(k) * SUB, SUB)
            outs[k][b, :local] = result[b, pl.ds(start, local * SUB), :].reshape(local, SUB, LANE)


def rates(plan, part, prepared, soot, acet, after, pieces, got):
    size = prepared[2].shape[0]
    local = size // plan.n
    sources, used = {}, []
    for (k, blocks), x in zip(pieces, got):
        if set(blocks) & set(part):
            for block in set(blocks) & set(part):
                sources[k, part.index(block)] = (len(used), blocks.index(block))
            used.append(x)
    shape = jax.ShapeDtypeStruct((len(part), local + 1, SUB, LANE), F32)
    return pl.pallas_call(
        functools.partial(rate_kernel, plan, sources, len(used), part),
        out_shape=[shape] * plan.n,
        in_specs=[VMEM] * 6 + [ANY] + [VMEM] * len(used),
        out_specs=[VMEM] * plan.n,
        scratch_shapes=[
            pltpu.VMEM((len(part), (SHIFTS + size) * SUB, LANE), F32),
            pltpu.VMEM((len(part), (size + 1) * SUB, LANE), F32),
            pltpu.VMEM((len(part), SUB, LANE), F32),
            pltpu.VMEM((2, GROUP, SHIFTS + SUB + size, LANE), F32),
        ],
        compiler_params=PARAMS,
        name="rates",
    )(*prepared, soot, acet, after, *used)


def near_kernel(given, after, out, sem):
    copy = pltpu.make_async_copy(given, out, sem)
    copy.start()
    copy.wait()


def near(soot, after):
    return pl.pallas_call(
        near_kernel,
        out_shape=jax.ShapeDtypeStruct(soot.shape, F32),
        in_specs=[HBM, ANY],
        out_specs=VMEM,
        scratch_shapes=[pltpu.SemaphoreType.DMA],
        compiler_params=PARAMS,
        name="near",
    )(pltpu.with_memory_space_constraint(soot, pltpu.HBM), after)


def gate(pieces, late):
    return pl.pallas_call(
        lambda *refs: None,
        out_shape=[jax.ShapeDtypeStruct(x.shape, x.dtype) for x in pieces],
        in_specs=[VMEM] * len(pieces) + [ANY] * len(late),
        out_specs=[VMEM] * len(pieces),
        input_output_aliases={i: i for i in range(len(pieces))},
        compiler_params=PARAMS,
        name="gate",
    )(*pieces, *late)


def base_kernel(diffusivity, kinetics, soot, species, soot_base, species_base):
    local, rows, width = soot.shape
    kinds = species.shape[0]
    lanes = lax.broadcasted_iota(jnp.int32, (rows, LANE), 1)
    none = jnp.zeros((1, width), F32)

    def spread(v, factor):
        up = jnp.concatenate([none, v[:-1]], axis=0)
        down = jnp.concatenate([v[1:], none], axis=0)
        left, right = pltpu.roll(v, 1, 1), pltpu.roll(v, width - 1, 1)
        left = jnp.concatenate([jnp.where(lanes == 0, 0.0, left[:, :LANE]), left[:, LANE:]], axis=1)
        right = jnp.concatenate([right[:, :-LANE], jnp.where(lanes == LANE - 1, 0.0, right[:, -LANE:])], axis=1)
        return (1.0 - 4.0 * factor) * v + factor * ((up + down) + (left + right))

    def one_section(i, carry):
        soot_base[i] = spread(soot[i], 0.1)
        return carry

    lax.fori_loop(0, local, one_section, 0, unroll=8)

    for row in range(0, rows, SUB):
        for col in range(0, width, 2 * LANE):
            tile = (slice(None), slice(row, row + SUB), slice(col, col + 2 * LANE))
            high, low = halves(species[tile].reshape(kinds * SUB, 2 * LANE))
            product = jnp.dot(kinetics[...], jnp.concatenate([high, low, high], axis=0), preferred_element_type=F32)
            species_base[tile] = product.reshape(kinds, SUB, 2 * LANE)

    def one_species(i, carry):
        species_base[i] += spread(species[i], diffusivity[i])
        return carry

    lax.fori_loop(0, kinds, one_species, 0, unroll=8)


def bases(diffusivity, kinetics, soot, species):
    return pl.pallas_call(
        base_kernel,
        out_shape=[jax.ShapeDtypeStruct(soot.shape, F32), jax.ShapeDtypeStruct(species.shape, F32)],
        in_specs=[SMEM, VMEM, VMEM, VMEM],
        out_specs=[VMEM, VMEM],
        compiler_params=PARAMS,
        name="bases",
    )(diffusivity, kinetics, soot, species)


def rim_kernel(inner, outer, diffusivity, soot_in, species_in, soot_base, species_base):
    local, rows, _ = soot_base.shape
    odd = lax.axis_index("xs") % 2 == 1
    for ref, at in ((soot_base, 0), (species_base, local)):
        for i in range(ref.shape[0]):
            factor = diffusivity[i] if at else 0.1
            one, other = inner[at + i : at + i + 1, :], outer[at + i : at + i + 1, :]
            ref[i, 0:1, :] += factor * jnp.where(odd, one, other)
            ref[i, rows - 1 : rows, :] += factor * jnp.where(odd, other, one)


def rim(inner, outer, diffusivity, soot_base, species_base):
    return pl.pallas_call(
        rim_kernel,
        out_shape=[jax.ShapeDtypeStruct(soot_base.shape, F32), jax.ShapeDtypeStruct(species_base.shape, F32)],
        in_specs=[VMEM, VMEM, SMEM, VMEM, VMEM],
        out_specs=[VMEM, VMEM],
        input_output_aliases={3: 0, 4: 1},
        compiler_params=PARAMS,
        name="rim",
    )(inner, outer, diffusivity, soot_base, species_base)


def last_kernel(plan, part, peers, stoich, soot_base, species_base, *refs):
    pieces = refs[: len(peers)]
    soot_out, species_out, soot_held, species_held, sems = refs[-5:]
    local, kinds = soot_out.shape[0], species_out.shape[0]
    units = [(k, b) for k in range(len(peers)) for b in range(len(part))]
    places = {(k, b): plan.place(peer(peers[k]), part[b]) for k, b in units}
    copies = []

    def send(source, target, sem):
        copies.append(pltpu.make_async_copy(source, target, sem))
        copies[-1].start()

    for k, b in units:
        rows, cols = places[k, b]
        soot_held[k, b] = soot_base[:, rows, cols] + pieces[k][b, :local]
        send(soot_held.at[k, b], soot_out.at[:, rows, cols], sems.at[0, k, b])
    used = {(k, b): pieces[k][b, local] for k, b in units}
    for kind in range(kinds):
        factor = stoich[kind]
        for k, b in units:
            rows, cols = places[k, b]
            species_held[k, b, kind] = species_base[kind, rows, cols] - factor * used[k, b]
    for k, b in units:
        rows, cols = places[k, b]
        send(species_held.at[k, b], species_out.at[:, rows, cols], sems.at[1, k, b])
    for copy in copies:
        copy.wait()


def last(plan, part, peers, stoich, soot_base, species_base, pieces, before):
    local, kinds = soot_base.shape[0], species_base.shape[0]
    first = 3 + len(pieces)
    return pl.pallas_call(
        functools.partial(last_kernel, plan, part, peers),
        out_shape=[jax.ShapeDtypeStruct(soot_base.shape, F32), jax.ShapeDtypeStruct(species_base.shape, F32)],
        in_specs=[SMEM, VMEM, VMEM] + [VMEM] * len(pieces) + [HBM] * len(before),
        out_specs=[HBM, HBM],
        scratch_shapes=[
            pltpu.VMEM((len(peers), len(part), local, SUB, LANE), F32),
            pltpu.VMEM((len(peers), len(part), kinds, SUB, LANE), F32),
            pltpu.SemaphoreType.DMA((2, len(peers), len(part))),
        ],
        input_output_aliases={first + i: i for i in range(len(before))},
        compiler_params=PARAMS,
        name="last",
    )(stoich, soot_base, species_base, *pieces, *before)


def shards(soot, species, kernel, split, target, growth, diffusivity, reaction, stoich):
    n = lax.axis_size("sec")
    count = lax.axis_size("xs")
    plan = Plan(n, soot.shape[1], soot.shape[2])

    def swap(x, k):
        return lax.ppermute(x, "sec", [(i, i ^ k) for i in range(n)])

    order = [k for k in (2, 1, 3) if k < n] + list(range(4, n))
    pieces = [(k, part) for k in order for part in plan.parts((0.75,) if k == n - 1 else ())]
    sent = cut(plan, pieces, soot)
    soot = near(soot, sent[0])
    got = [swap(x, k) for (k, _), x in zip(pieces, sent)]

    inner, outer = edges(soot, species, sent[0])
    pairs = [[(i, i + 1) for i in range(first, count - 1, 2)] for first in (0, 1)]
    inner, outer = (lax.ppermute(x, "xs", [q for i, j in p for q in ((i, j), (j, i))]) for x, p in zip((inner, outer), pairs))
    *prepared, kinetics = weights(plan, kernel, split, target, growth, reaction)
    base = bases(diffusivity, kinetics, soot, species)
    base = rim(inner, outer, diffusivity, *base)

    back = []
    for part in plan.parts((0.5,)):
        outs = rates(plan, part, prepared, soot, species, base[0] if not back else stoich, pieces, got)
        late = [x for (_, blocks), x in zip(pieces, got) if not set(blocks) & set(part)]
        away = gate(outs[1:], late) if late else outs[1:]
        back.append((part, [outs[0]] + [swap(x, k) for k, x in enumerate(away, 1)]))
    result = ()
    for i, (part, moved) in enumerate(back):
        early = 2 if i == len(back) - 1 else n
        for peers in (range(early), range(early, n)):
            if peers:
                result = last(plan, part, peers, stoich, *base, [moved[k] for k in peers], result)
    return tuple(result)


def solution(mesh):
    return jax.shard_map(
        shards,
        mesh=mesh,
        in_specs=(P("sec", "xs", None), P(None, "xs", None), P(), P(), P(), P(), P(), P(), P()),
        out_specs=(P("sec", "xs", None), P(None, "xs", None)),
        check_vma=False,
    )
```

```python
import functools

import jax
import jax.numpy as jnp
from jax import lax
from jax.experimental import pallas as pl
from jax.experimental.pallas import tpu as pltpu
from jax.sharding import PartitionSpec as P

F32 = jnp.float32
BF16 = jnp.bfloat16
SUB = 8
LANE = 128
GROUP = 2
SHIFTS = 5
ANY = pl.BlockSpec(memory_space=pl.ANY)
VMEM = pl.BlockSpec(memory_space=pltpu.VMEM)
SMEM = pl.BlockSpec(memory_space=pltpu.SMEM)
HBM = pl.BlockSpec(memory_space=pltpu.HBM)
PARAMS = pltpu.CompilerParams(vmem_limit_bytes=16 * 1024 * 1024)


def halves(x):
    high = x.astype(BF16)
    return high, (x - high.astype(F32)).astype(BF16)


class Plan:
    def __init__(self, n, rows, width):
        self.n = n
        self.across = min(n, width // LANE)
        self.rows = rows // (n // self.across)
        self.cols = width // self.across
        self.blocks = [(r, c) for r in range(self.rows // SUB) for c in range(self.cols // LANE)]

    def parts(self, ends):
        stops = [round(end * len(self.blocks)) for end in ends]
        whole = list(range(len(self.blocks)))
        return [p for p in (whole[x:y] for x, y in zip([0] + stops, stops + [None])) if p]

    def place(self, owner, block):
        r, c = self.blocks[block]
        row = (owner // self.across) * self.rows + r * SUB
        col = (owner % self.across) * self.cols + c * LANE
        return pl.ds(pl.multiple_of(row, SUB), SUB), pl.ds(pl.multiple_of(col, LANE), LANE)


def peer(k):
    return lax.axis_index("sec") ^ k


def cut_kernel(plan, pieces, soot, *rest):
    outs, sem = rest[:-1], rest[-1]
    copies = []
    for out, (k, part) in zip(outs, pieces):
        for b, block in enumerate(part):
            rows, cols = plan.place(peer(k), block)
            copies.append(pltpu.make_async_copy(soot.at[:, rows, cols], out.at[b], sem.at[len(copies)]))
            copies[-1].start()
    for copy in copies:
        copy.wait()


def cut(plan, pieces, soot):
    shapes = [jax.ShapeDtypeStruct((len(part), soot.shape[0], SUB, LANE), F32) for _, part in pieces]
    return pl.pallas_call(
        functools.partial(cut_kernel, plan, pieces),
        out_shape=shapes,
        in_specs=[HBM],
        out_specs=[VMEM] * len(shapes),
        scratch_shapes=[pltpu.SemaphoreType.DMA((sum(len(part) for _, part in pieces),))],
        compiler_params=PARAMS,
        name="cut",
    )(pltpu.with_memory_space_constraint(soot, pltpu.HBM))


def edge_kernel(soot, species, after, inner, outer):
    local, rows, _ = soot.shape
    odd = lax.axis_index("xs") % 2 == 1
    for ref, at in ((soot, 0), (species, local)):
        count = ref.shape[0]
        head, tail = ref[:, 0, :], ref[:, rows - 1, :]
        inner[at : at + count, :] = jnp.where(odd, head, tail)
        outer[at : at + count, :] = jnp.where(odd, tail, head)


def edges(soot, species, after):
    shape = jax.ShapeDtypeStruct((soot.shape[0] + species.shape[0], soot.shape[2]), F32)
    return pl.pallas_call(
        edge_kernel,
        out_shape=[shape, shape],
        in_specs=[VMEM, VMEM, ANY],
        out_specs=[VMEM, VMEM],
        compiler_params=PARAMS,
        name="edges",
    )(soot, species, after)


def weight_kernel(kernel, split, target, growth, reaction, lower, upper, rate, rate_before, spread_out, scratch):
    size = kernel.shape[0]
    row = lax.broadcasted_iota(jnp.int32, (size, size), 0)
    col = lax.broadcasted_iota(jnp.int32, (size, size), 1)
    k, sp = kernel[...], split[...]
    t = target[...].astype(F32)
    rowf = row.astype(F32)
    k_t, sp_t, t_t = k.T, sp.T, t.T
    low, high = 0.5 * k * sp, 0.5 * k * (1.0 - sp)
    low_t, high_t = 0.5 * k_t * sp_t, 0.5 * k_t * (1.0 - sp_t)

    def fed(shift):
        at = rowf + shift
        own = jnp.where(t == at, low, 0.0) + jnp.where(t + 1.0 == at, high, 0.0)
        other = jnp.where(t_t == at, low_t, 0.0) + jnp.where(t_t + 1.0 == at, high_t, 0.0)
        return jnp.where(col <= row, own, 0.0) + jnp.where(col < row, other, 0.0)

    scratch[...] = jnp.zeros_like(scratch)
    scratch[0:size, :] = fed(0) - k
    for shift in range(1, SHIFTS):
        scratch[shift * size + shift : (shift + 1) * size, :] = fed(shift)[: size - shift]
    last = SHIFTS * size
    scratch[last : last + SUB - 1, :] = fed(-1)[size - SUB + 1 :]
    w_high, w_low = halves(scratch[...])
    most = size - 2 * SUB
    for i in range(1, SHIFTS):
        at = slice(most * (i - 1), most * i)
        for j, part in enumerate((w_high, w_high, w_low)):
            lower[at, most * j : most * (j + 1)] = part[i * size : i * size + most, :most]
    rest = [slice(0, size)] + [slice(i * size + most, (i + 1) * size) for i in range(1, SHIFTS)] + [slice(last, last + 2 * SUB)]
    at = 0
    for rows in rest:
        count = rows.stop - rows.start
        for j, part in enumerate((w_high, w_high, w_low)):
            upper[at : at + count, size * j : size * (j + 1)] = part[rows]
        at += count
    diagonal = jnp.where(row == col, jnp.broadcast_to(growth[...], (size, size)), 0.0)
    column = jnp.sum(diagonal, axis=1, keepdims=True)
    rate[...] = jnp.broadcast_to(column, rate.shape)
    before = jnp.where(row == col + 1, jnp.broadcast_to(growth[...], (size, size)), 0.0)
    column = jnp.sum(before, axis=1, keepdims=True)
    rate_before[...] = jnp.broadcast_to(column, rate_before.shape)


    kinds = reaction.shape[0]
    wide = kinds * SUB
    tall = lax.broadcasted_iota(jnp.int32, (wide, kinds), 0) // SUB == lax.broadcasted_iota(jnp.int32, (wide, kinds), 1)
    flat = lax.broadcasted_iota(jnp.int32, (kinds, wide), 1) // SUB == lax.broadcasted_iota(jnp.int32, (kinds, wide), 0)
    tall, flat = tall.astype(F32).astype(BF16), flat.astype(F32).astype(BF16)
    same = lax.broadcasted_iota(jnp.int32, (wide, wide), 0) % SUB == lax.broadcasted_iota(jnp.int32, (wide, wide), 1) % SUB
    wider = []
    for half in halves(reaction[...]):
        rows = jnp.dot(tall, half, preferred_element_type=F32).astype(BF16)
        wider.append(jnp.where(same, jnp.dot(rows, flat, preferred_element_type=F32), 0.0))
    spread_out[...] = jnp.concatenate([wider[0], wider[0], wider[1]], axis=1).astype(BF16)


def weights(plan, kernel, split, target, growth, reaction):
    size, kinds = kernel.shape[0], reaction.shape[0]
    depth = SHIFTS * size + 2 * SUB
    return pl.pallas_call(
        weight_kernel,
        out_shape=[
            jax.ShapeDtypeStruct(((SHIFTS - 1) * (size - 2 * SUB), 3 * (size - 2 * SUB)), BF16),
            jax.ShapeDtypeStruct((size + 2 * SUB * SHIFTS, 3 * size), BF16),
            jax.ShapeDtypeStruct((size, GROUP * LANE), F32),
            jax.ShapeDtypeStruct((size, GROUP * LANE), F32),
            jax.ShapeDtypeStruct((kinds * SUB, 3 * kinds * SUB), BF16),
        ],
        in_specs=[VMEM] * 5,
        out_specs=[VMEM] * 5,
        scratch_shapes=[pltpu.VMEM((depth, size), F32)],
        compiler_params=PARAMS,
        name="weights",
    )(kernel, split, target, growth.reshape(1, size), reaction)


def rate_kernel(plan, sources, count, part, lower, upper, rate, rate_before, soot, acet, after, *refs):
    n = plan.n
    pieces, outs = refs[:count], refs[count : count + n]
    whole, result, near, shifted = refs[count + n :]
    size = rate.shape[0]
    local = size // n
    for b, block in enumerate(part):
        rows, cols = plan.place(lax.axis_index("sec"), block)
        near[b] = acet[0, rows, cols]
    pad, most = SHIFTS - 1, size - 2 * SUB
    for b in range(len(part)):
        whole[b, : pad * SUB, :] = jnp.zeros((pad * SUB, LANE), F32)
        whole[b, (pad + size) * SUB :, :] = jnp.zeros((SUB, LANE), F32)
        for k in range(n):
            start = pl.multiple_of((pad + local * peer(k)) * SUB, SUB)
            if k:
                source, at = sources[k, b]
                piece = pieces[source][at]
            else:
                rows, cols = plan.place(lax.axis_index("sec"), part[b])
                piece = soot[:, rows, cols]
            whole[b, pl.ds(start, local * SUB), :] = piece.reshape(local * SUB, LANE)
    def sections(first, count, pair):
        found = [whole[b, pl.ds((pad + first) * SUB + row, count, stride=SUB), :] for b, row in pair]
        return jnp.concatenate(found, axis=1)

    units = [(b, row) for row in range(SUB) for b in range(len(part))]
    for i in range(GROUP):
        shifted[:, i, :pad, :] = jnp.zeros((2, pad, LANE), F32)
        shifted[:, i, pad + size :, :] = jnp.zeros((2, SHIFTS + SUB - pad, LANE), F32)
    for step, pair in enumerate([units[i : i + GROUP] for i in range(0, len(units), GROUP)]):
        here = sections(0, size, pair)
        moved = shifted.at[step % 2]
        for i in range(GROUP):
            moved[i, pad : pad + size, :] = here[:, i * LANE : (i + 1) * LANE]

        def near_by(first, count):
            return jnp.concatenate([moved[i, pad + first : pad + first + count, :] for i in range(GROUP)], axis=1)

        high, low = halves(here)
        product = jnp.dot(upper[...], jnp.concatenate([high, low, high], axis=0), preferred_element_type=F32)
        high, low = high[:most], low[:most]
        below = jnp.dot(lower[...], jnp.concatenate([high, low, high], axis=0), preferred_element_type=F32)
        total = here * product[:size]
        for shift in range(1, SHIFTS):
            moved_here = near_by(-shift, size)
            before = moved_here if shift == 1 else before
            top = size + 2 * SUB * (shift - 1)
            total += moved_here * jnp.concatenate([below[most * (shift - 1) : most * shift], product[top : top + 2 * SUB]], axis=0)
        last = size + 2 * SUB * (SHIFTS - 1)
        extra = near_by(size - SUB + 1, SUB) * product[last : last + SUB]
        total = jnp.concatenate([total[: size - SUB], total[size - SUB :] + extra], axis=0)
        growing = jnp.concatenate([near[b, row : row + 1, :] for b, row in pair], axis=1)
        grown = rate[...] * here
        total -= growing * (grown - rate_before[...] * before)
        used = growing * jnp.sum(grown, axis=0, keepdims=True)
        for i, (b, row) in enumerate(pair):
            lanes = slice(i * LANE, (i + 1) * LANE)
            result[b, pl.ds(row, size, stride=SUB), :] = total[:, lanes]
            for k in range(n):
                outs[k][b, local, row : row + 1, :] = used[:, lanes]
    for b in range(len(part)):
        for k in range(n):
            start = pl.multiple_of(local * peer(k) * SUB, SUB)
            outs[k][b, :local] = result[b, pl.ds(start, local * SUB), :].reshape(local, SUB, LANE)


def rates(plan, part, prepared, soot, acet, after, pieces, got):
    size = prepared[2].shape[0]
    local = size // plan.n
    sources, used = {}, []
    for (k, blocks), x in zip(pieces, got):
        if set(blocks) & set(part):
            for block in set(blocks) & set(part):
                sources[k, part.index(block)] = (len(used), blocks.index(block))
            used.append(x)
    shape = jax.ShapeDtypeStruct((len(part), local + 1, SUB, LANE), F32)
    return pl.pallas_call(
        functools.partial(rate_kernel, plan, sources, len(used), part),
        out_shape=[shape] * plan.n,
        in_specs=[VMEM] * 6 + [ANY] + [VMEM] * len(used),
        out_specs=[VMEM] * plan.n,
        scratch_shapes=[
            pltpu.VMEM((len(part), (SHIFTS + size) * SUB, LANE), F32),
            pltpu.VMEM((len(part), (size + 1) * SUB, LANE), F32),
            pltpu.VMEM((len(part), SUB, LANE), F32),
            pltpu.VMEM((2, GROUP, SHIFTS + SUB + size, LANE), F32),
        ],
        compiler_params=PARAMS,
        name="rates",
    )(*prepared, soot, acet, after, *used)


def near_kernel(given, after, out, sem):
    copy = pltpu.make_async_copy(given, out, sem)
    copy.start()
    copy.wait()


def near(soot, after):
    return pl.pallas_call(
        near_kernel,
        out_shape=jax.ShapeDtypeStruct(soot.shape, F32),
        in_specs=[HBM, ANY],
        out_specs=VMEM,
        scratch_shapes=[pltpu.SemaphoreType.DMA],
        compiler_params=PARAMS,
        name="near",
    )(pltpu.with_memory_space_constraint(soot, pltpu.HBM), after)


def gate(pieces, late):
    return pl.pallas_call(
        lambda *refs: None,
        out_shape=[jax.ShapeDtypeStruct(x.shape, x.dtype) for x in pieces],
        in_specs=[VMEM] * len(pieces) + [ANY] * len(late),
        out_specs=[VMEM] * len(pieces),
        input_output_aliases={i: i for i in range(len(pieces))},
        compiler_params=PARAMS,
        name="gate",
    )(*pieces, *late)


def base_kernel(diffusivity, kinetics, soot, species, soot_base, species_base):
    local, rows, width = soot.shape
    kinds = species.shape[0]
    lanes = lax.broadcasted_iota(jnp.int32, (rows, LANE), 1)
    none = jnp.zeros((1, width), F32)

    def spread(v, factor):
        up = jnp.concatenate([none, v[:-1]], axis=0)
        down = jnp.concatenate([v[1:], none], axis=0)
        left, right = pltpu.roll(v, 1, 1), pltpu.roll(v, width - 1, 1)
        left = jnp.concatenate([jnp.where(lanes == 0, 0.0, left[:, :LANE]), left[:, LANE:]], axis=1)
        right = jnp.concatenate([right[:, :-LANE], jnp.where(lanes == LANE - 1, 0.0, right[:, -LANE:])], axis=1)
        return (1.0 - 4.0 * factor) * v + factor * ((up + down) + (left + right))

    def one_section(i, carry):
        soot_base[i] = spread(soot[i], 0.1)
        return carry

    lax.fori_loop(0, local, one_section, 0, unroll=True)

    for row in range(0, rows, SUB):
        for col in range(0, width, 2 * LANE):
            tile = (slice(None), slice(row, row + SUB), slice(col, col + 2 * LANE))
            high, low = halves(species[tile].reshape(kinds * SUB, 2 * LANE))
            product = jnp.dot(kinetics[...], jnp.concatenate([high, low, high], axis=0), preferred_element_type=F32)
            species_base[tile] = product.reshape(kinds, SUB, 2 * LANE)

    def one_species(i, carry):
        species_base[i] += spread(species[i], diffusivity[i])
        return carry

    lax.fori_loop(0, kinds, one_species, 0, unroll=True)


def bases(diffusivity, kinetics, soot, species):
    return pl.pallas_call(
        base_kernel,
        out_shape=[jax.ShapeDtypeStruct(soot.shape, F32), jax.ShapeDtypeStruct(species.shape, F32)],
        in_specs=[SMEM, VMEM, VMEM, VMEM],
        out_specs=[VMEM, VMEM],
        compiler_params=PARAMS,
        name="bases",
    )(diffusivity, kinetics, soot, species)


def rim_kernel(inner, outer, diffusivity, soot_in, species_in, soot_base, species_base):
    local, rows, _ = soot_base.shape
    odd = lax.axis_index("xs") % 2 == 1
    for ref, at in ((soot_base, 0), (species_base, local)):
        for i in range(ref.shape[0]):
            factor = diffusivity[i] if at else 0.1
            one, other = inner[at + i : at + i + 1, :], outer[at + i : at + i + 1, :]
            ref[i, 0:1, :] += factor * jnp.where(odd, one, other)
            ref[i, rows - 1 : rows, :] += factor * jnp.where(odd, other, one)


def rim(inner, outer, diffusivity, soot_base, species_base):
    return pl.pallas_call(
        rim_kernel,
        out_shape=[jax.ShapeDtypeStruct(soot_base.shape, F32), jax.ShapeDtypeStruct(species_base.shape, F32)],
        in_specs=[VMEM, VMEM, SMEM, VMEM, VMEM],
        out_specs=[VMEM, VMEM],
        input_output_aliases={3: 0, 4: 1},
        compiler_params=PARAMS,
        name="rim",
    )(inner, outer, diffusivity, soot_base, species_base)


def last_kernel(plan, part, peers, stoich, soot_base, species_base, *refs):
    pieces = refs[: len(peers)]
    soot_out, species_out, soot_held, species_held, sems = refs[-5:]
    local, kinds = soot_out.shape[0], species_out.shape[0]
    units = [(k, b) for k in range(len(peers)) for b in range(len(part))]
    places = {(k, b): plan.place(peer(peers[k]), part[b]) for k, b in units}
    copies = []

    def send(source, target, sem):
        copies.append(pltpu.make_async_copy(source, target, sem))
        copies[-1].start()

    for k, b in units:
        rows, cols = places[k, b]
        soot_held[k, b] = soot_base[:, rows, cols] + pieces[k][b, :local]
        send(soot_held.at[k, b], soot_out.at[:, rows, cols], sems.at[0, k, b])
    used = {(k, b): pieces[k][b, local] for k, b in units}
    for kind in range(kinds):
        factor = stoich[kind]
        for k, b in units:
            rows, cols = places[k, b]
            species_held[k, b, kind] = species_base[kind, rows, cols] - factor * used[k, b]
    for k, b in units:
        rows, cols = places[k, b]
        send(species_held.at[k, b], species_out.at[:, rows, cols], sems.at[1, k, b])
    for copy in copies:
        copy.wait()


def last(plan, part, peers, stoich, soot_base, species_base, pieces, before):
    local, kinds = soot_base.shape[0], species_base.shape[0]
    first = 3 + len(pieces)
    return pl.pallas_call(
        functools.partial(last_kernel, plan, part, peers),
        out_shape=[jax.ShapeDtypeStruct(soot_base.shape, F32), jax.ShapeDtypeStruct(species_base.shape, F32)],
        in_specs=[SMEM, VMEM, VMEM] + [VMEM] * len(pieces) + [HBM] * len(before),
        out_specs=[HBM, HBM],
        scratch_shapes=[
            pltpu.VMEM((len(peers), len(part), local, SUB, LANE), F32),
            pltpu.VMEM((len(peers), len(part), kinds, SUB, LANE), F32),
            pltpu.SemaphoreType.DMA((2, len(peers), len(part))),
        ],
        input_output_aliases={first + i: i for i in range(len(before))},
        compiler_params=PARAMS,
        name="last",
    )(stoich, soot_base, species_base, *pieces, *before)


def shards(soot, species, kernel, split, target, growth, diffusivity, reaction, stoich):
    n = lax.axis_size("sec")
    count = lax.axis_size("xs")
    plan = Plan(n, soot.shape[1], soot.shape[2])

    def swap(x, k):
        return lax.ppermute(x, "sec", [(i, i ^ k) for i in range(n)])

    order = [k for k in (2, 1, 3) if k < n] + list(range(4, n))
    pieces = [(k, part) for k in order for part in plan.parts((0.75,) if k == n - 1 else ())]
    sent = cut(plan, pieces, soot)
    soot = near(soot, sent[0])
    got = [swap(x, k) for (k, _), x in zip(pieces, sent)]

    inner, outer = edges(soot, species, sent[0])
    pairs = [[(i, i + 1) for i in range(first, count - 1, 2)] for first in (0, 1)]
    inner, outer = (lax.ppermute(x, "xs", [q for i, j in p for q in ((i, j), (j, i))]) for x, p in zip((inner, outer), pairs))
    *prepared, kinetics = weights(plan, kernel, split, target, growth, reaction)
    base = bases(diffusivity, kinetics, soot, species)
    base = rim(inner, outer, diffusivity, *base)

    back = []
    for part in plan.parts((0.5,)):
        outs = rates(plan, part, prepared, soot, species, base[0] if not back else stoich, pieces, got)
        late = [x for (_, blocks), x in zip(pieces, got) if not set(blocks) & set(part)]
        away = [*outs[1 : n - 1], *gate(outs[n - 1 :], late)] if late else outs[1:]
        back.append((part, [outs[0]] + [swap(x, k) for k, x in enumerate(away, 1)]))
    result = ()
    for i, (part, moved) in enumerate(back):
        early = 2 if i == len(back) - 1 else n
        for peers in (range(early), range(early, n)):
            if peers:
                result = last(plan, part, peers, stoich, *base, [moved[k] for k in peers], result)
    return tuple(result)


def solution(mesh):
    return jax.shard_map(
        shards,
        mesh=mesh,
        in_specs=(P("sec", "xs", None), P(None, "xs", None), P(), P(), P(), P(), P(), P(), P()),
        out_specs=(P("sec", "xs", None), P(None, "xs", None)),
        check_vma=False,
    )
```

```python
import functools

import jax
import jax.numpy as jnp
from jax import lax
from jax.experimental import pallas as pl
from jax.experimental.pallas import tpu as pltpu
from jax.sharding import PartitionSpec as P

F32 = jnp.float32
BF16 = jnp.bfloat16
SUB = 8
LANE = 128
GROUP = 2
SHIFTS = 5
ANY = pl.BlockSpec(memory_space=pl.ANY)
VMEM = pl.BlockSpec(memory_space=pltpu.VMEM)
SMEM = pl.BlockSpec(memory_space=pltpu.SMEM)
HBM = pl.BlockSpec(memory_space=pltpu.HBM)
PARAMS = pltpu.CompilerParams(vmem_limit_bytes=16 * 1024 * 1024)


def halves(x):
    high = x.astype(BF16)
    return high, (x - high.astype(F32)).astype(BF16)


class Plan:
    def __init__(self, n, rows, width):
        self.n = n
        self.across = min(n, width // LANE)
        self.rows = rows // (n // self.across)
        self.cols = width // self.across
        self.blocks = [(r, c) for r in range(self.rows // SUB) for c in range(self.cols // LANE)]

    def parts(self, ends):
        stops = [round(end * len(self.blocks)) for end in ends]
        whole = list(range(len(self.blocks)))
        return [p for p in (whole[x:y] for x, y in zip([0] + stops, stops + [None])) if p]

    def place(self, owner, block):
        r, c = self.blocks[block]
        row = (owner // self.across) * self.rows + r * SUB
        col = (owner % self.across) * self.cols + c * LANE
        return pl.ds(pl.multiple_of(row, SUB), SUB), pl.ds(pl.multiple_of(col, LANE), LANE)


def peer(k):
    return lax.axis_index("sec") ^ k


def cut_kernel(plan, pieces, soot, *rest):
    outs, sem = rest[:-1], rest[-1]
    copies = []
    for out, (k, part) in zip(outs, pieces):
        for b, block in enumerate(part):
            rows, cols = plan.place(peer(k), block)
            copies.append(pltpu.make_async_copy(soot.at[:, rows, cols], out.at[b], sem.at[len(copies)]))
            copies[-1].start()
    for copy in copies:
        copy.wait()


def cut(plan, pieces, soot):
    shapes = [jax.ShapeDtypeStruct((len(part), soot.shape[0], SUB, LANE), F32) for _, part in pieces]
    return pl.pallas_call(
        functools.partial(cut_kernel, plan, pieces),
        out_shape=shapes,
        in_specs=[HBM],
        out_specs=[VMEM] * len(shapes),
        scratch_shapes=[pltpu.SemaphoreType.DMA((sum(len(part) for _, part in pieces),))],
        compiler_params=PARAMS,
        name="cut",
    )(pltpu.with_memory_space_constraint(soot, pltpu.HBM))


def edge_kernel(soot, species, after, inner, outer):
    local, rows, _ = soot.shape
    odd = lax.axis_index("xs") % 2 == 1
    for ref, at in ((soot, 0), (species, local)):
        count = ref.shape[0]
        head, tail = ref[:, 0, :], ref[:, rows - 1, :]
        inner[at : at + count, :] = jnp.where(odd, head, tail)
        outer[at : at + count, :] = jnp.where(odd, tail, head)


def edges(soot, species, after):
    shape = jax.ShapeDtypeStruct((soot.shape[0] + species.shape[0], soot.shape[2]), F32)
    return pl.pallas_call(
        edge_kernel,
        out_shape=[shape, shape],
        in_specs=[VMEM, VMEM, ANY],
        out_specs=[VMEM, VMEM],
        compiler_params=PARAMS,
        name="edges",
    )(soot, species, after)


def weight_kernel(kernel, split, target, growth, reaction, lower, upper, rate, rate_before, spread_out, scratch):
    size = kernel.shape[0]
    row = lax.broadcasted_iota(jnp.int32, (size, size), 0)
    col = lax.broadcasted_iota(jnp.int32, (size, size), 1)
    k, sp = kernel[...], split[...]
    t = target[...].astype(F32)
    rowf = row.astype(F32)
    k_t, sp_t, t_t = k.T, sp.T, t.T
    low, high = 0.5 * k * sp, 0.5 * k * (1.0 - sp)
    low_t, high_t = 0.5 * k_t * sp_t, 0.5 * k_t * (1.0 - sp_t)

    def fed(shift):
        at = rowf + shift
        own = jnp.where(t == at, low, 0.0) + jnp.where(t + 1.0 == at, high, 0.0)
        other = jnp.where(t_t == at, low_t, 0.0) + jnp.where(t_t + 1.0 == at, high_t, 0.0)
        return jnp.where(col <= row, own, 0.0) + jnp.where(col < row, other, 0.0)

    scratch[...] = jnp.zeros_like(scratch)
    scratch[0:size, :] = fed(0) - k
    for shift in range(1, SHIFTS):
        scratch[shift * size + shift : (shift + 1) * size, :] = fed(shift)[: size - shift]
    last = SHIFTS * size
    scratch[last : last + SUB - 1, :] = fed(-1)[size - SUB + 1 :]
    w_high, w_low = halves(scratch[...])
    most = size - 2 * SUB
    for i in range(1, SHIFTS):
        at = slice(most * (i - 1), most * i)
        for j, part in enumerate((w_high, w_high, w_low)):
            lower[at, most * j : most * (j + 1)] = part[i * size : i * size + most, :most]
    rest = [slice(0, size)] + [slice(i * size + most, (i + 1) * size) for i in range(1, SHIFTS)] + [slice(last, last + 2 * SUB)]
    at = 0
    for rows in rest:
        count = rows.stop - rows.start
        for j, part in enumerate((w_high, w_high, w_low)):
            upper[at : at + count, size * j : size * (j + 1)] = part[rows]
        at += count
    diagonal = jnp.where(row == col, jnp.broadcast_to(growth[...], (size, size)), 0.0)
    column = jnp.sum(diagonal, axis=1, keepdims=True)
    rate[...] = jnp.broadcast_to(column, rate.shape)
    before = jnp.where(row == col + 1, jnp.broadcast_to(growth[...], (size, size)), 0.0)
    column = jnp.sum(before, axis=1, keepdims=True)
    rate_before[...] = jnp.broadcast_to(column, rate_before.shape)


    kinds = reaction.shape[0]
    wide = kinds * SUB
    tall = lax.broadcasted_iota(jnp.int32, (wide, kinds), 0) // SUB == lax.broadcasted_iota(jnp.int32, (wide, kinds), 1)
    flat = lax.broadcasted_iota(jnp.int32, (kinds, wide), 1) // SUB == lax.broadcasted_iota(jnp.int32, (kinds, wide), 0)
    tall, flat = tall.astype(F32).astype(BF16), flat.astype(F32).astype(BF16)
    same = lax.broadcasted_iota(jnp.int32, (wide, wide), 0) % SUB == lax.broadcasted_iota(jnp.int32, (wide, wide), 1) % SUB
    wider = []
    for half in halves(reaction[...]):
        rows = jnp.dot(tall, half, preferred_element_type=F32).astype(BF16)
        wider.append(jnp.where(same, jnp.dot(rows, flat, preferred_element_type=F32), 0.0))
    spread_out[...] = jnp.concatenate([wider[0], wider[0], wider[1]], axis=1).astype(BF16)


def weights(plan, kernel, split, target, growth, reaction):
    size, kinds = kernel.shape[0], reaction.shape[0]
    depth = SHIFTS * size + 2 * SUB
    return pl.pallas_call(
        weight_kernel,
        out_shape=[
            jax.ShapeDtypeStruct(((SHIFTS - 1) * (size - 2 * SUB), 3 * (size - 2 * SUB)), BF16),
            jax.ShapeDtypeStruct((size + 2 * SUB * SHIFTS, 3 * size), BF16),
            jax.ShapeDtypeStruct((size, GROUP * LANE), F32),
            jax.ShapeDtypeStruct((size, GROUP * LANE), F32),
            jax.ShapeDtypeStruct((kinds * SUB, 3 * kinds * SUB), BF16),
        ],
        in_specs=[VMEM] * 5,
        out_specs=[VMEM] * 5,
        scratch_shapes=[pltpu.VMEM((depth, size), F32)],
        compiler_params=PARAMS,
        name="weights",
    )(kernel, split, target, growth.reshape(1, size), reaction)


def rate_kernel(plan, sources, count, part, lower, upper, rate, rate_before, soot, acet, after, *refs):
    n = plan.n
    pieces, outs = refs[:count], refs[count : count + n]
    whole, result, near, shifted = refs[count + n :]
    size = rate.shape[0]
    local = size // n
    for b, block in enumerate(part):
        rows, cols = plan.place(lax.axis_index("sec"), block)
        near[b] = acet[0, rows, cols]
    pad, most = SHIFTS - 1, size - 2 * SUB
    for b in range(len(part)):
        whole[b, : pad * SUB, :] = jnp.zeros((pad * SUB, LANE), F32)
        whole[b, (pad + size) * SUB :, :] = jnp.zeros((SUB, LANE), F32)
        for k in range(n):
            start = pl.multiple_of((pad + local * peer(k)) * SUB, SUB)
            if k:
                source, at = sources[k, b]
                piece = pieces[source][at]
            else:
                rows, cols = plan.place(lax.axis_index("sec"), part[b])
                piece = soot[:, rows, cols]
            whole[b, pl.ds(start, local * SUB), :] = piece.reshape(local * SUB, LANE)
    def sections(first, count, pair):
        found = [whole[b, pl.ds((pad + first) * SUB + row, count, stride=SUB), :] for b, row in pair]
        return jnp.concatenate(found, axis=1)

    units = [(b, row) for row in range(SUB) for b in range(len(part))]
    for i in range(GROUP):
        shifted[:, i, :pad, :] = jnp.zeros((2, pad, LANE), F32)
        shifted[:, i, pad + size :, :] = jnp.zeros((2, SHIFTS + SUB - pad, LANE), F32)
    for step, pair in enumerate([units[i : i + GROUP] for i in range(0, len(units), GROUP)]):
        here = sections(0, size, pair)
        moved = shifted.at[step % 2]
        for i in range(GROUP):
            moved[i, pad : pad + size, :] = here[:, i * LANE : (i + 1) * LANE]

        def near_by(first, count):
            return jnp.concatenate([moved[i, pad + first : pad + first + count, :] for i in range(GROUP)], axis=1)

        high, low = halves(here)
        product = jnp.dot(upper[...], jnp.concatenate([high, low, high], axis=0), preferred_element_type=F32)
        high, low = high[:most], low[:most]
        below = jnp.dot(lower[...], jnp.concatenate([high, low, high], axis=0), preferred_element_type=F32)
        total = here * product[:size]
        for shift in range(1, SHIFTS):
            moved_here = near_by(-shift, size)
            before = moved_here if shift == 1 else before
            top = size + 2 * SUB * (shift - 1)
            total += moved_here * jnp.concatenate([below[most * (shift - 1) : most * shift], product[top : top + 2 * SUB]], axis=0)
        last = size + 2 * SUB * (SHIFTS - 1)
        extra = near_by(size - SUB + 1, SUB) * product[last : last + SUB]
        total = jnp.concatenate([total[: size - SUB], total[size - SUB :] + extra], axis=0)
        growing = jnp.concatenate([near[b, row : row + 1, :] for b, row in pair], axis=1)
        grown = rate[...] * here
        total -= growing * (grown - rate_before[...] * before)
        used = growing * jnp.sum(grown, axis=0, keepdims=True)
        for i, (b, row) in enumerate(pair):
            lanes = slice(i * LANE, (i + 1) * LANE)
            result[b, pl.ds(row, size, stride=SUB), :] = total[:, lanes]
            for k in range(n):
                outs[k][b, local, row : row + 1, :] = used[:, lanes]
    for b in range(len(part)):
        for k in range(n):
            start = pl.multiple_of(local * peer(k) * SUB, SUB)
            outs[k][b, :local] = result[b, pl.ds(start, local * SUB), :].reshape(local, SUB, LANE)


def rates(plan, part, prepared, soot, acet, after, pieces, got):
    size = prepared[2].shape[0]
    local = size // plan.n
    sources, used = {}, []
    for (k, blocks), x in zip(pieces, got):
        if set(blocks) & set(part):
            for block in set(blocks) & set(part):
                sources[k, part.index(block)] = (len(used), blocks.index(block))
            used.append(x)
    shape = jax.ShapeDtypeStruct((len(part), local + 1, SUB, LANE), F32)
    return pl.pallas_call(
        functools.partial(rate_kernel, plan, sources, len(used), part),
        out_shape=[shape] * plan.n,
        in_specs=[VMEM] * 6 + [ANY] + [VMEM] * len(used),
        out_specs=[VMEM] * plan.n,
        scratch_shapes=[
            pltpu.VMEM((len(part), (SHIFTS + size) * SUB, LANE), F32),
            pltpu.VMEM((len(part), (size + 1) * SUB, LANE), F32),
            pltpu.VMEM((len(part), SUB, LANE), F32),
            pltpu.VMEM((2, GROUP, SHIFTS + SUB + size, LANE), F32),
        ],
        compiler_params=PARAMS,
        name="rates",
    )(*prepared, soot, acet, after, *used)


def near_kernel(given, after, out, sem):
    copy = pltpu.make_async_copy(given, out, sem)
    copy.start()
    copy.wait()


def near(soot, after):
    return pl.pallas_call(
        near_kernel,
        out_shape=jax.ShapeDtypeStruct(soot.shape, F32),
        in_specs=[HBM, ANY],
        out_specs=VMEM,
        scratch_shapes=[pltpu.SemaphoreType.DMA],
        compiler_params=PARAMS,
        name="near",
    )(pltpu.with_memory_space_constraint(soot, pltpu.HBM), after)


def gate(pieces, late):
    return pl.pallas_call(
        lambda *refs: None,
        out_shape=[jax.ShapeDtypeStruct(x.shape, x.dtype) for x in pieces],
        in_specs=[VMEM] * len(pieces) + [ANY] * len(late),
        out_specs=[VMEM] * len(pieces),
        input_output_aliases={i: i for i in range(len(pieces))},
        compiler_params=PARAMS,
        name="gate",
    )(*pieces, *late)


def base_kernel(diffusivity, kinetics, soot, species, soot_base, species_base):
    local, rows, width = soot.shape
    kinds = species.shape[0]
    lanes = lax.broadcasted_iota(jnp.int32, (rows, LANE), 1)
    none = jnp.zeros((1, width), F32)

    def spread(v, factor):
        up = jnp.concatenate([none, v[:-1]], axis=0)
        down = jnp.concatenate([v[1:], none], axis=0)
        left, right = pltpu.roll(v, 1, 1), pltpu.roll(v, width - 1, 1)
        left = jnp.concatenate([jnp.where(lanes == 0, 0.0, left[:, :LANE]), left[:, LANE:]], axis=1)
        right = jnp.concatenate([right[:, :-LANE], jnp.where(lanes == LANE - 1, 0.0, right[:, -LANE:])], axis=1)
        return (1.0 - 4.0 * factor) * v + factor * ((up + down) + (left + right))

    def one_section(i, carry):
        soot_base[i] = spread(soot[i], 0.1)
        return carry

    lax.fori_loop(0, local, one_section, 0, unroll=True)

    for row in range(0, rows, SUB):
        for col in range(0, width, 2 * LANE):
            tile = (slice(None), slice(row, row + SUB), slice(col, col + 2 * LANE))
            high, low = halves(species[tile].reshape(kinds * SUB, 2 * LANE))
            product = jnp.dot(kinetics[...], jnp.concatenate([high, low, high], axis=0), preferred_element_type=F32)
            species_base[tile] = product.reshape(kinds, SUB, 2 * LANE)

    def one_species(i, carry):
        species_base[i] += spread(species[i], diffusivity[i])
        return carry

    lax.fori_loop(0, kinds, one_species, 0, unroll=True)


def bases(diffusivity, kinetics, soot, species):
    return pl.pallas_call(
        base_kernel,
        out_shape=[jax.ShapeDtypeStruct(soot.shape, F32), jax.ShapeDtypeStruct(species.shape, F32)],
        in_specs=[SMEM, VMEM, VMEM, VMEM],
        out_specs=[VMEM, VMEM],
        compiler_params=PARAMS,
        name="bases",
    )(diffusivity, kinetics, soot, species)


def rim_kernel(inner, outer, diffusivity, soot_in, species_in, soot_base, species_base):
    local, rows, _ = soot_base.shape
    odd = lax.axis_index("xs") % 2 == 1
    for ref, at in ((soot_base, 0), (species_base, local)):
        for i in range(ref.shape[0]):
            factor = diffusivity[i] if at else 0.1
            one, other = inner[at + i : at + i + 1, :], outer[at + i : at + i + 1, :]
            ref[i, 0:1, :] += factor * jnp.where(odd, one, other)
            ref[i, rows - 1 : rows, :] += factor * jnp.where(odd, other, one)


def rim(inner, outer, diffusivity, soot_base, species_base):
    return pl.pallas_call(
        rim_kernel,
        out_shape=[jax.ShapeDtypeStruct(soot_base.shape, F32), jax.ShapeDtypeStruct(species_base.shape, F32)],
        in_specs=[VMEM, VMEM, SMEM, VMEM, VMEM],
        out_specs=[VMEM, VMEM],
        input_output_aliases={3: 0, 4: 1},
        compiler_params=PARAMS,
        name="rim",
    )(inner, outer, diffusivity, soot_base, species_base)


def last_kernel(plan, part, peers, stoich, soot_base, species_base, *refs):
    pieces = refs[: len(peers)]
    soot_out, species_out, soot_held, species_held, sems = refs[-5:]
    local, kinds = soot_out.shape[0], species_out.shape[0]
    units = [(k, b) for k in range(len(peers)) for b in range(len(part))]
    places = {(k, b): plan.place(peer(peers[k]), part[b]) for k, b in units}
    copies = []

    def send(source, target, sem):
        copies.append(pltpu.make_async_copy(source, target, sem))
        copies[-1].start()

    for k, b in units:
        rows, cols = places[k, b]
        soot_held[k, b] = soot_base[:, rows, cols] + pieces[k][b, :local]
        send(soot_held.at[k, b], soot_out.at[:, rows, cols], sems.at[0, k, b])
    used = {(k, b): pieces[k][b, local] for k, b in units}
    for kind in range(kinds):
        factor = stoich[kind]
        for k, b in units:
            rows, cols = places[k, b]
            species_held[k, b, kind] = species_base[kind, rows, cols] - factor * used[k, b]
    for k, b in units:
        rows, cols = places[k, b]
        send(species_held.at[k, b], species_out.at[:, rows, cols], sems.at[1, k, b])
    for copy in copies:
        copy.wait()


def last(plan, part, peers, stoich, soot_base, species_base, pieces, before):
    local, kinds = soot_base.shape[0], species_base.shape[0]
    first = 3 + len(pieces)
    return pl.pallas_call(
        functools.partial(last_kernel, plan, part, peers),
        out_shape=[jax.ShapeDtypeStruct(soot_base.shape, F32), jax.ShapeDtypeStruct(species_base.shape, F32)],
        in_specs=[SMEM, VMEM, VMEM] + [VMEM] * len(pieces) + [HBM] * len(before),
        out_specs=[HBM, HBM],
        scratch_shapes=[
            pltpu.VMEM((len(peers), len(part), local, SUB, LANE), F32),
            pltpu.VMEM((len(peers), len(part), kinds, SUB, LANE), F32),
            pltpu.SemaphoreType.DMA((2, len(peers), len(part))),
        ],
        input_output_aliases={first + i: i for i in range(len(before))},
        compiler_params=PARAMS,
        name="last",
    )(stoich, soot_base, species_base, *pieces, *before)


def shards(soot, species, kernel, split, target, growth, diffusivity, reaction, stoich):
    n = lax.axis_size("sec")
    count = lax.axis_size("xs")
    plan = Plan(n, soot.shape[1], soot.shape[2])

    def swap(x, k):
        return lax.ppermute(x, "sec", [(i, i ^ k) for i in range(n)])

    order = [k for k in (2, 1, 3) if k < n] + list(range(4, n))
    pieces = [(k, part) for k in order for part in plan.parts((0.75,) if k == n - 1 else ())]
    sent = cut(plan, pieces, soot)
    soot = near(soot, sent[0])
    got = [swap(x, k) for (k, _), x in zip(pieces, sent)]

    inner, outer = edges(soot, species, sent[0])
    pairs = [[(i, i + 1) for i in range(first, count - 1, 2)] for first in (0, 1)]
    inner, outer = (lax.ppermute(x, "xs", [q for i, j in p for q in ((i, j), (j, i))]) for x, p in zip((inner, outer), pairs))
    *prepared, kinetics = weights(plan, kernel, split, target, growth, reaction)
    base = bases(diffusivity, kinetics, soot, species)
    base = rim(inner, outer, diffusivity, *base)

    back = []
    for part in plan.parts((0.5,)):
        outs = rates(plan, part, prepared, soot, species, base[0] if not back else stoich, pieces, got)
        late = [x for (_, blocks), x in zip(pieces, got) if not set(blocks) & set(part)]
        away = [*outs[1 : n - 1], *gate(outs[n - 1 :], late)] if late else outs[1:]
        back.append((part, [outs[0]] + [swap(x, k) for k, x in enumerate(away, 1)]))
    result = ()
    for i, (part, moved) in enumerate(back):
        early = 2 if i == len(back) - 1 else n
        groups = (range(early), range(early, n)) if early == n or n < 4 else ([0, 2], [1, *range(3, n)])
        for peers in groups:
            if peers:
                result = last(plan, part, peers, stoich, *base, [moved[k] for k in peers], result)
    return tuple(result)


def solution(mesh):
    return jax.shard_map(
        shards,
        mesh=mesh,
        in_specs=(P("sec", "xs", None), P(None, "xs", None), P(), P(), P(), P(), P(), P(), P()),
        out_specs=(P("sec", "xs", None), P(None, "xs", None)),
        check_vma=False,
    )
```
